256 devices in a mesh: dp: 2 (over z_lo), seq: 128 (over x, z_hi, y, core).
Axes of the slice: x: 4, y: 4, z: 8 (z_hi: 4, z_lo: 2; z = z_hi * 2 + z_lo), core: 2. Of those that a mesh axis runs over, the one named last changes fastest.
Arguments:
- frames: bfloat16 [2, 32768, 256], P('dp', 'seq'), may hold values from -6 to 6
- upstream: bfloat16 [2, 256, 256, 256], P('dp', 'seq'), may hold values from -6 to 6
- intra_weights: bfloat16 [4, 256, 256], replicated, may hold values from -0.375 to 0.375
- inter_weights: bfloat16 [4, 256, 256], replicated, may hold values from -0.375 to 0.375
- gains: float32 [2, 256], replicated, may hold values from 0.5 to 1.5
Outputs:
- grad_frames: bfloat16 [2, 32768, 256], P('dp', 'seq')
- grad_intra: float32 [4, 256, 256], replicated
- grad_inter: float32 [4, 256, 256], replicated
- grad_gains: float32 [2, 256], replicated
The draws below stay inside these ranges and needn't reach their ends.
All inputs are finite; a program needn't handle non-finite values.
Results may differ from the reference program's by a relative error of at most 0.025.
Values may be sent and summed in bfloat16 or wider, within the bound.
A program may use at most 64 MiB of HBM per device.

```python
import jax
import jax.numpy as jnp
from jax import lax

N = 256
H = 8
K = 256
HOP = 128
CH_DEV = 2
S = 256
FR = 32768
MIX = 2


def block_levels(own_key, extent, pieces, least, largest):
    factor_of, own = 1.0, jax.random.fold_in(own_key, 6)
    for position, shards_of in pieces:
        draws = jnp.exp(jax.random.uniform(jax.random.fold_in(own, position), (shards_of,), jnp.float32, least / len(pieces), largest / len(pieces)))
        factor_of = factor_of * jnp.repeat(draws, extent[position] // shards_of).reshape([-1 if axis == position else 1 for axis in range(len(extent))])
    return factor_of


def normal_values(rng, extent, scale, reach, pieces=(), kind=jnp.bfloat16):
    gain = block_levels(rng, extent, pieces, -0.22, 0.18) if pieces else 1.0
    values = jax.random.normal(rng, extent, jnp.float32) * scale * gain
    return jnp.minimum(jnp.maximum(values, -reach), reach).astype(kind)


def setup_inputs(seed: int = 0) -> dict:
    key_of = jax.random.split(jax.random.key(seed), 6)
    frames = normal_values(key_of[0], (MIX, FR, N), 1.0, 6.0, ((0, 2), (1, 128)))
    upstream = normal_values(key_of[1], (MIX, K, S, N), 1.0, 6.0, ((0, 2), (1, 128)))
    intra_weights = normal_values(key_of[2], (4, N, N), N ** -0.5, 0.375)
    inter_weights = normal_values(key_of[3], (4, N, N), N ** -0.5, 0.375)
    gains = jnp.clip(1.0 + 0.1 * jax.random.normal(key_of[4], (2, N), jnp.float32), 0.5, 1.5)
    return dict(frames=frames, upstream=upstream, intra_weights=intra_weights, inter_weights=inter_weights, gains=gains)


epsilon = 1e-05

def product(form, left, right):
    return jnp.einsum(form, left.astype(jnp.float32), right.astype(jnp.float32))

def layer_forward(source, matrices, scaling):
    groups, length, width = source.shape
    head_size = width // H
    values_f = source.astype(jnp.float32)
    centred = values_f - lax.optimization_barrier(jnp.mean(values_f, -1, keepdims=True))
    inverse = lax.rsqrt(lax.optimization_barrier(jnp.mean(centred * centred, -1, keepdims=True)) + epsilon)
    normed = centred * inverse
    hidden = (normed * scaling).astype(jnp.bfloat16)
    projected = product('gln,cnm->cglm', hidden, matrices[:3]).astype(jnp.bfloat16)
    queries = projected[0].reshape(groups, length, H, head_size)
    key_rows = projected[1].reshape(groups, length, H, head_size)
    value_rows = projected[2].reshape(groups, length, H, head_size)
    scores = product('glhd,gmhd->ghlm', queries, key_rows) * head_size ** (-0.5)
    attend = jax.nn.softmax(scores, axis=-1)
    rounded = attend.astype(jnp.bfloat16)
    combined = product('ghlm,gmhd->glhd', rounded, value_rows).astype(jnp.bfloat16).reshape(groups, length, width)
    result = values_f + product('gln,nm->glm', combined, matrices[3])
    saved = (normed, inverse, hidden, queries, key_rows, value_rows, rounded, attend, combined)
    return (result, saved)

def layer_backward(saved, upstream, matrices, scaling):
    normed, inverse, hidden, queries, key_rows, value_rows, rounded, attend, combined = saved
    groups, length, width = upstream.shape
    head_size = width // H
    grad_out = product('gln,glm->nm', combined, upstream)
    grad_comb = product('glm,nm->gln', upstream, matrices[3]).astype(jnp.bfloat16).reshape(groups, length, H, head_size)
    grad_attend = product('glhd,gmhd->ghlm', grad_comb, value_rows)
    grad_values = product('ghlm,glhd->gmhd', rounded, grad_comb).astype(jnp.bfloat16)
    grad_scores = (attend * (grad_attend - lax.optimization_barrier(jnp.sum(grad_attend * attend, -1, keepdims=True))) * head_size ** (-0.5)).astype(jnp.bfloat16)
    grad_queries = product('ghlm,gmhd->glhd', grad_scores, key_rows).astype(jnp.bfloat16)
    grad_keys = product('ghlm,glhd->gmhd', grad_scores, queries).astype(jnp.bfloat16)
    grad_proj = jnp.stack([grad_queries, grad_keys, grad_values]).reshape(3, groups, length, width)
    grad_mats = product('gln,cglm->cnm', hidden, grad_proj)
    grad_hidden = product('cglm,cnm->gln', grad_proj, matrices[:3])
    grad_gain = lax.optimization_barrier(jnp.sum(grad_hidden * normed, axis=(0, 1)))
    grad_normed = grad_hidden * scaling
    grad_norm = inverse * (grad_normed - lax.optimization_barrier(jnp.mean(grad_normed, -1, keepdims=True)) - normed * lax.optimization_barrier(jnp.mean(grad_normed * normed, -1, keepdims=True)))
    grad_source = upstream.astype(jnp.float32) + grad_norm
    return (grad_source, jnp.concatenate([grad_mats, grad_out[None]], 0), grad_gain)

def reference(frames, upstream, intra_weights, inter_weights, gains):
    padded = jnp.pad(frames, ((0, 0), (0, HOP), (0, 0))).reshape(MIX, S + 1, HOP, N)
    spans = jnp.concatenate([padded[:, :-1], padded[:, 1:]], axis=2)
    blocks = spans.reshape(-1, CH_DEV, K, N)

    def intra_only(block):
        return layer_forward(block, intra_weights, gains[0])[0].astype(jnp.bfloat16)
    inner = lax.map(intra_only, blocks)
    inner = inner.reshape(MIX, S, K, N).transpose(0, 2, 1, 3).reshape(MIX * K, S, N)
    upper = upstream.reshape(MIX * K, S, N)

    def inter_step(totals, inputs):
        source, grad_top = inputs
        result, saved = layer_forward(source[None], inter_weights, gains[1])
        grad_source, grad_mats, grad_gain = layer_backward(saved, grad_top[None], inter_weights, gains[1])
        return ((totals[0] + grad_mats, totals[1] + grad_gain), grad_source[0].astype(jnp.bfloat16))
    start = (jnp.zeros((4, N, N), jnp.float32), jnp.zeros((N,), jnp.float32))
    (grad_inter, gain_inter), grad_inner = lax.scan(inter_step, start, (inner, upper))
    grad_inner = grad_inner.reshape(MIX, K, S, N).transpose(0, 2, 1, 3).reshape(-1, CH_DEV, K, N)

    def intra_step(totals, inputs):
        block, grad_top = inputs
        result, saved = layer_forward(block, intra_weights, gains[0])
        grad_source, grad_mats, grad_gain = layer_backward(saved, grad_top, intra_weights, gains[0])
        return ((totals[0] + grad_mats, totals[1] + grad_gain), grad_source)
    (grad_intra, gain_intra), grad_spans = lax.scan(intra_step, start, (blocks, grad_inner))
    grad_spans = grad_spans.reshape(MIX, S, K, N)
    first_half = grad_spans[:, :, :HOP]
    second_half = grad_spans[:, :, HOP:]
    summed = first_half.at[:, 1:].add(second_half[:, :-1])
    grad_frames = summed.reshape(MIX, FR, N).astype(jnp.bfloat16)
    return (grad_frames, grad_intra, grad_inter, jnp.stack([gain_intra, gain_inter]))
```

```python
import functools

import jax
import jax.numpy as jnp
from jax import lax
from jax.experimental import pallas as pl
from jax.experimental.pallas import tpu as pltpu
from jax.sharding import PartitionSpec as P

MESH = pl.DeviceIdType.MESH
bf16, f32 = jnp.bfloat16, jnp.float32

H = 8
D = 32
N = 256
R = 256
NR = 8
NG = 16
EPS = 1e-05
C = D**-0.5
LOG2E = 1.4426950408889634


def mm(a, b):
    return jnp.dot(a, b, preferred_element_type=f32)


def head_mask(h):
    lane = lax.broadcasted_iota(jnp.int32, (1, N), 1)
    return jnp.where((lane >= D * h) & (lane < D * (h + 1)), 1.0, 0.0).astype(bf16)


def forward(x, w, gain, s, i, want_out):
    cen = x - jnp.mean(x, -1, keepdims=True)
    inv = lax.rsqrt(jnp.mean(cen * cen, -1, keepdims=True) + EPS)
    normed = cen * inv
    s["normed"][i] = normed
    s["inv"][i] = inv
    hidden = (normed * gain).astype(bf16)
    s["hiddenT"][:, i * R : (i + 1) * R] = hidden.T
    q = mm(hidden, w[0])
    s["q"][i] = q.astype(bf16)
    s["qT"][i] = (q * (C * LOG2E)).astype(bf16).T
    k = mm(hidden, w[1]).astype(bf16)
    s["k"][i] = k
    s["kT"][i] = k.T
    v = mm(hidden, w[2]).astype(bf16)
    s["v"][i] = v
    s["vT"][i] = v.T
    for h in range(H):
        rows = slice(D * h, D * (h + 1))
        scores = mm(s["k"][i] * head_mask(h), s["qT"][i])
        p = jnp.exp2(scores - jnp.max(scores, 0, keepdims=True))
        a = (p * (1.0 / jnp.sum(p, 0, keepdims=True))).astype(bf16)
        s["A"][i, :, h * R : (h + 1) * R] = a
        s["combT"][i, rows, :] = mm(s["vT"][i, rows, :], a)
    if want_out:
        return x + mm(s["combT"][i].astype(bf16).T, w[3])
    return None


def backward(g, w3T, wT, gain, s, i):
    gc = mm(g, w3T[...]).astype(bf16)
    s["gcT"][...] = gc.T
    for h in range(H):
        mask = head_mask(h)
        rows = slice(D * h, D * (h + 1))
        cols = slice(h * R, (h + 1) * R)
        s["gcs"][cols, :] = gc * mask
        s["qs"][cols, :] = s["q"][i] * mask
        ga = mm(s["v"][i] * mask, s["gcT"][...])
        drow = jnp.sum(s["gcT"][rows, :].astype(f32) * s["combT"][i, rows, :], 0, keepdims=True)
        d = (s["A"][i, :, cols].astype(f32) * (ga - drow)).astype(bf16)
        s["Dm"][:, cols] = d
        s["gqT"][rows, :] = (mm(s["kT"][i, rows, :], d) * C).astype(bf16)
    gv = mm(s["A"][i], s["gcs"][...]).astype(bf16)
    gk = (mm(s["Dm"][...], s["qs"][...]) * C).astype(bf16)
    gqkv = jnp.concatenate([s["gqT"][...].T, gk, gv], axis=1)
    s["gqkv"][i * R : (i + 1) * R, :] = gqkv
    gh = mm(gqkv, wT[...])
    normed = s["normed"][i]
    ggain = jnp.sum(gh * normed, 0, keepdims=True)
    t = gh * gain
    dx = g.astype(f32) + s["inv"][i] * (
        t - jnp.mean(t, -1, keepdims=True) - normed * jnp.mean(t * normed, -1, keepdims=True)
    )
    return dx, ggain


def saved_scratch():
    def square(kind):
        return pltpu.VMEM((2, R, N), kind)

    return dict(
        normed=square(f32),
        inv=pltpu.VMEM((2, R, 1), f32),
        hiddenT=pltpu.VMEM((N, 2 * R), bf16),
        q=square(bf16),
        qT=square(bf16),
        k=square(bf16),
        kT=square(bf16),
        v=square(bf16),
        vT=square(bf16),
        A=pltpu.VMEM((2, R, H * R), bf16),
        combT=square(f32),
        gqkv=pltpu.VMEM((2 * R, 3 * N), bf16),
    )


def shared_scratch():
    return dict(
        gcT=pltpu.VMEM((N, R), bf16),
        gcs=pltpu.VMEM((H * R, N), bf16),
        qs=pltpu.VMEM((H * R, N), bf16),
        Dm=pltpu.VMEM((R, H * R), bf16),
        gqT=pltpu.VMEM((N, R), bf16),
    )


def weight_scratch():
    return dict(wT=pltpu.VMEM((3 * N, N), bf16), w3T=pltpu.VMEM((N, N), bf16))


def comm_scratch():
    dma = pltpu.SemaphoreType.DMA
    block = pltpu.VMEM((2, NG, 16, N), bf16)
    near = pltpu.VMEM((NR, 2, 2, 16, N), bf16)
    bufs = dict(
        halo=pltpu.VMEM((R // 2, N), bf16),
        tail=pltpu.VMEM((R // 2, N), bf16),
        tail_in=pltpu.VMEM((R // 2, N), bf16),
        a_out=block,
        a_in=block,
        b_out=pltpu.VMEM((2, NR, 2, 16, N), bf16),
        b_in=near,
        rb_out=pltpu.VMEM((2, NR, 2, 16, N), bf16),
        rb_in=near,
        ra_out=block,
        ra_in=block,
        s1_out=pltpu.VMEM((2, NR, 144, N), bf16),
        s1_in=pltpu.VMEM((2, NR, 144, N), bf16),
        s2_out=pltpu.VMEM((2, NG, 32, 128), bf16),
        s2_in=pltpu.VMEM((2, NG, 32, 128), bf16),
        s3_out=pltpu.VMEM((2, 32, 128), f32),
        s3_in=pltpu.VMEM((2, 32, 128), f32),
        g2=pltpu.VMEM((2, NG, 16, 128), bf16),
        g1=pltpu.VMEM((2, NR, 128, N), bf16),
    )
    sems = {}
    for name, shape in dict(
        halo=(1, 1),
        tail=(1, 1),
        a=(2, NG),
        b=(2, NR),
        rb=(2, NR),
        ra=(2, NG),
        s1=(2, NR),
        s2=(2, NG),
        s3=(2, 1),
        g2=(2, NG),
        g1=(2, NR),
    ).items():
        sems[name + "_send"] = dma(shape)
        sems[name + "_recv"] = dma(shape)
    return bufs, sems


def loop(lo, hi, f):
    def step(d, carry):
        f(d)
        return carry

    lax.fori_loop(lo, hi, step, 0)


def kernel(n_seq, frames, upstream, w1, w2, gains, gf, gw1, gw2, gg, s1, s2, shared, wt1, wt2, bufs, sems):
    s1, s2 = dict(s1, **shared), dict(s2, **shared)
    me, dp = lax.axis_index("seq"), lax.axis_index("dp")
    g, r = lax.div(me, NR), lax.rem(me, NR)
    right, left = lax.rem(me + 1, n_seq), lax.rem(me + n_seq - 1, n_seq)

    def far(gg_):
        return {"seq": gg_ * NR + r}

    def near(rr):
        return {"seq": g * NR + rr}

    def ahead(d, n, mine):
        return lax.rem(mine + d, n)

    def behind(d, n, mine):
        return lax.rem(mine + n - d, n)

    def copy(name, c, d, src, dst, to):
        return pltpu.make_async_remote_copy(
            src_ref=src,
            dst_ref=dst,
            send_sem=sems[name + "_send"].at[c, d],
            recv_sem=sems[name + "_recv"].at[c, d],
            device_id=to,
            device_id_type=MESH,
        )

    class Exchange:
        def __init__(self, name, c, n, mine, address, src, dst):
            self.n = n

            def out(d):
                peer = ahead(d, n, mine)
                return copy(name, c, d, src(peer), dst(mine), address(peer))

            def came(d):
                peer = behind(d, n, mine)
                return copy(name, c, d, src(peer), dst(peer), address(peer))

            self.out, self.came = out, came

        def start(self):
            loop(1, self.n, lambda d: self.out(d).start())

        def wait_recv(self):
            loop(1, self.n, lambda d: self.came(d).wait_recv())

        def wait_send(self):
            loop(1, self.n, lambda d: self.out(d).wait_send())

    def far_exchange(name, c, src, dst):
        return Exchange(name, c, NG, g, far, src, dst)

    def near_exchange(name, c, src, dst):
        return Exchange(name, c, NR, r, near, src, dst)

    b = bufs
    ex_a = [far_exchange("a", c, lambda p, c=c: b["a_out"].at[c, p], lambda p, c=c: b["a_in"].at[c, p]) for c in range(2)]
    ex_b = [near_exchange("b", c, lambda p, c=c: b["b_out"].at[c, p], lambda p, c=c: b["b_in"].at[p, c]) for c in range(2)]
    ex_rb = [near_exchange("rb", c, lambda p, c=c: b["rb_out"].at[c, p], lambda p, c=c: b["rb_in"].at[p, c]) for c in range(2)]
    ex_ra = [far_exchange("ra", c, lambda p, c=c: b["ra_out"].at[c, p], lambda p, c=c: b["ra_in"].at[c, p]) for c in range(2)]
    ex_s1 = [near_exchange("s1", c, lambda p, c=c: b["s1_out"].at[c, p], lambda p, c=c: b["s1_in"].at[c, p]) for c in range(2)]
    ex_s2 = [far_exchange("s2", c, lambda p, c=c: b["s2_out"].at[c, p], lambda p, c=c: b["s2_in"].at[c, p]) for c in range(2)]
    ex_g2 = [far_exchange("g2", c, lambda p, c=c: b["g2"].at[c, g], lambda p, c=c: b["g2"].at[c, p]) for c in range(2)]
    ex_g1 = [near_exchange("g1", c, lambda p, c=c: b["g1"].at[c, r], lambda p, c=c: b["g1"].at[c, p]) for c in range(2)]
    ex_s3 = [copy("s3", c, 0, b["s3_out"].at[c], b["s3_in"].at[c], {"dp": 1 - dp}) for c in range(2)]

    barrier = pltpu.get_barrier_semaphore()

    def greet(device):
        pl.semaphore_signal(barrier, inc=1, device_id=device, device_id_type=MESH)

    loop(1, NG, lambda d: greet(far(ahead(d, NG, g))))
    loop(1, NR, lambda d: greet(near(ahead(d, NR, r))))
    greet({"seq": right})
    greet({"seq": left})
    greet({"dp": 1 - dp})

    row = lax.broadcasted_iota(jnp.int32, (R, R), 0)
    col = lax.broadcasted_iota(jnp.int32, (R, R), 1)
    swap = jnp.where((row % 16) * 16 + row // 16 == col, 1.0, 0.0).astype(bf16)

    def swapped(x):
        return mm(swap, x).astype(bf16)

    for w, wt in ((w1, wt1), (w2, wt2)):
        for j in range(3):
            wt["wT"][j * N : (j + 1) * N, :] = w[j].T
        wt["w3T"][...] = w[3].T
    g1, g2 = gains[0:1], gains[1:2]

    pl.semaphore_wait(barrier, NG - 1 + NR - 1 + 3)
    halo = copy("halo", 0, 0, frames.at[0, 0 : R // 2], b["halo"], {"seq": left})
    halo.start()

    def spread(c, out):
        out = out.astype(bf16).reshape(NG, 16, N)
        b["a_out"][c] = out
        ex_a[c].start()
        b["a_in"][c, g] = b["a_out"][c, g]

    def regroup(c):
        ex_a[c].wait_recv()
        b["b_out"][c] = swapped(b["a_in"][c].reshape(R, N)).reshape(NR, 2, 16, N)
        ex_b[c].start()
        b["b_in"][r, c] = b["b_out"][c, r]

    own = frames[0].astype(f32)
    spread(0, forward(own, w1, g1, s1, 0, True))
    halo.wait_recv()
    following = jnp.where(me < n_seq - 1, b["halo"][...].astype(f32), 0.0)
    out1 = forward(jnp.concatenate([own[R // 2 :], following], 0), w1, g1, s1, 1, True)
    regroup(0)
    spread(1, out1)
    upper = [swapped(upstream[0, i]) for i in range(2)]
    regroup(1)
    for c in range(2):
        ex_b[c].wait_recv()

    gain2 = jnp.zeros((1, N), f32)
    g3 = jnp.zeros((N, N), f32)
    for i in range(2):
        forward(b["b_in"][:, :, i].reshape(R, N).astype(f32), w2, g2, s2, i, False)
        dx, gain = backward(upper[i], wt2["w3T"], wt2["wT"], g2, s2, i)
        gain2 += gain
        b["rb_out"][i] = dx.astype(bf16).reshape(NR, 2, 16, N)
        ex_rb[i].start()
        b["rb_in"][r, i] = b["rb_out"][i, r]
        g3 += mm(s2["combT"][i].astype(bf16), upper[i])

    row16 = lax.broadcasted_iota(jnp.int32, (16, 1), 0)

    def two_rows(x):
        high = x.astype(bf16).astype(f32)
        return jnp.where(row16 == 0, high, jnp.where(row16 == 1, x - high, 0.0))

    def sum_start(a, proj, out, gain):
        for j in range(4):
            m = out if j == 3 else proj[:, j * N : (j + 1) * N]
            b["s1_out"][a, 2 * j : 2 * j + 2, 0:128, :] = m.astype(bf16).reshape(2, 128, N)
        rows = two_rows(gain).astype(bf16)
        for p in range(NR):
            b["s1_out"][a, p, 128:144, :] = rows
        ex_s1[a].start()
        b["s1_in"][a, r] = b["s1_out"][a, r]

    def sum_second(a):
        ex_s1[a].wait_recv()
        total = b["s1_in"][a, 0].astype(f32)
        for p in range(1, NR):
            total += b["s1_in"][a, p].astype(f32)
        gain = total[128:129] + total[129:130]
        rows = two_rows(gain)
        rows = rows[:, 0:128] + jnp.where(
            row16 == 2, rows[0:1, 128:256], jnp.where(row16 == 3, rows[1:2, 128:256], 0.0)
        )
        rows = rows.astype(bf16)
        for p in range(NG):
            i, j = p // 2, p % 2
            b["s2_out"][a, p, 0:16] = total[16 * i : 16 * i + 16, 128 * j : 128 * j + 128].astype(bf16)
            b["s2_out"][a, p, 16:32] = rows
        ex_s2[a].start()
        b["s2_in"][a, g] = b["s2_out"][a, g]

    def sum_third(a):
        ex_s2[a].wait_recv()
        total = b["s2_in"][a, 0].astype(f32)
        for p in range(1, NG):
            total += b["s2_in"][a, p].astype(f32)
        b["s3_out"][a] = total
        ex_s3[a].start()

    def sum_fourth(a):
        ex_s3[a].wait_recv()
        total = b["s3_out"][a] + b["s3_in"][a]
        b["g2"][a, g] = total[0:16].astype(bf16)
        ex_g2[a].start()
        gg[a : a + 1, 0:128] = total[16:17] + total[17:18]
        gg[a : a + 1, 128:256] = total[18:19] + total[19:20]

    def sum_fifth(a):
        ex_g2[a].wait_recv()
        for p in range(NG):
            i, j = p // 2, p % 2
            b["g1"][a, r, 16 * i : 16 * i + 16, 128 * j : 128 * j + 128] = b["g2"][a, p]
        ex_g1[a].start()

    def sum_finish(a, gw):
        ex_g1[a].wait_recv()
        for p in range(NR):
            gw[p // 2, 128 * (p % 2) : 128 * (p % 2) + 128, :] = b["g1"][a, p].astype(f32)

    for c in range(2):
        ex_rb[c].wait_recv()
    for c in (1, 0):
        back = b["rb_in"][:, :, c].reshape(R, N)
        b["ra_out"][c] = swapped(back).reshape(NG, 16, N)
        ex_ra[c].start()
        b["ra_in"][c, g] = b["ra_out"][c, g]
    sum_start(1, mm(s2["hiddenT"][...], s2["gqkv"][...]), g3, gain2)

    ex_ra[1].wait_recv()
    top1 = b["ra_in"][1].reshape(R, N)
    dx1, gain1 = backward(top1, wt1["w3T"], wt1["wT"], g1, s1, 1)
    b["tail"][...] = dx1[R // 2 :].astype(bf16)
    tail = copy("tail", 0, 0, b["tail"], b["tail_in"], {"seq": right})
    tail.start()
    sum_second(1)
    ex_ra[0].wait_recv()
    top0 = b["ra_in"][0].reshape(R, N)
    g3 = mm(s1["combT"][0].astype(bf16), top0) + mm(s1["combT"][1].astype(bf16), top1)
    dx0, gain0 = backward(top0, wt1["w3T"], wt1["wT"], g1, s1, 0)
    sum_start(0, mm(s1["hiddenT"][...], s1["gqkv"][...]), g3, gain0 + gain1)
    tail.wait_recv()
    carried = jnp.where(me > 0, b["tail_in"][...].astype(f32), 0.0)
    gf[0, 0 : R // 2] = (dx0[0 : R // 2] + carried).astype(bf16)
    gf[0, R // 2 :] = (dx0[R // 2 :] + dx1[0 : R // 2]).astype(bf16)
    sum_third(1)
    sum_second(0)
    sum_fourth(1)
    sum_third(0)
    sum_fifth(1)
    sum_fourth(0)
    sum_fifth(0)
    sum_finish(1, gw2)
    sum_finish(0, gw1)

    halo.wait_send()
    tail.wait_send()
    for group in (ex_a, ex_b, ex_rb, ex_ra, ex_s1, ex_s2, ex_s3, ex_g2, ex_g1):
        for c in range(2):
            group[c].wait_send()


def on_device(n_seq, frames, upstream, w1, w2, gains):
    vmem = pl.BlockSpec(memory_space=pltpu.VMEM)
    bufs, sems = comm_scratch()
    return pl.pallas_call(
        functools.partial(kernel, n_seq),
        in_specs=[vmem] * 5,
        out_specs=[vmem] * 4,
        out_shape=[
            jax.ShapeDtypeStruct(frames.shape, bf16),
            jax.ShapeDtypeStruct(w1.shape, f32),
            jax.ShapeDtypeStruct(w2.shape, f32),
            jax.ShapeDtypeStruct(gains.shape, f32),
        ],
        scratch_shapes=[
            saved_scratch(),
            saved_scratch(),
            shared_scratch(),
            weight_scratch(),
            weight_scratch(),
            bufs,
            sems,
        ],
        compiler_params=pltpu.CompilerParams(
            collective_id=0, has_side_effects=True, vmem_limit_bytes=56 * 2**20
        ),
        name="block_backward",
    )(frames, upstream, w1, w2, gains)


def solution(mesh):
    placed = (P("dp", "seq", None), P("dp", "seq", None, None), P(), P(), P())
    return jax.shard_map(
        functools.partial(on_device, mesh.shape["seq"]),
        mesh=mesh,
        in_specs=placed,
        out_specs=(P("dp", "seq", None), P(), P(), P()),
        check_vma=False,
    )
```

```python
import functools

import jax
import jax.numpy as jnp
from jax import lax
from jax.experimental import pallas as pl
from jax.experimental.pallas import tpu as pltpu
from jax.sharding import PartitionSpec as P

MESH = pl.DeviceIdType.MESH
bf16, f32 = jnp.bfloat16, jnp.float32

H = 8
D = 32
N = 256
R = 256
NR = 8
NG = 16
X, ZH, Y, CORE = 4, 4, 4, 2
DP = 2
Z = ZH * DP
EPS = 1e-05
C = D**-0.5
LOG2E = 1.4426950408889634


def mm(a, b):
    return jnp.dot(a, b, preferred_element_type=f32)


def head_mask(h):
    lane = lax.broadcasted_iota(jnp.int32, (1, N), 1)
    return jnp.where((lane >= D * h) & (lane < D * (h + 1)), 1.0, 0.0).astype(bf16)


def forward(x, w, gain, s, i, want_out):
    cen = x - jnp.mean(x, -1, keepdims=True)
    inv = lax.rsqrt(jnp.mean(cen * cen, -1, keepdims=True) + EPS)
    normed = cen * inv
    s["normed"][i] = normed
    s["inv"][i] = inv
    hidden = (normed * gain).astype(bf16)
    s["hiddenT"][:, i * R : (i + 1) * R] = hidden.T
    q = mm(hidden, w[0])
    s["q"][i] = q.astype(bf16)
    s["qT"][i] = (q * (C * LOG2E)).astype(bf16).T
    k = mm(hidden, w[1]).astype(bf16)
    s["k"][i] = k
    s["kT"][i] = k.T
    v = mm(hidden, w[2]).astype(bf16)
    s["v"][i] = v
    s["vT"][i] = v.T
    for h in range(H):
        rows = slice(D * h, D * (h + 1))
        scores = mm(s["k"][i] * head_mask(h), s["qT"][i])
        p = jnp.exp2(scores - jnp.max(scores, 0, keepdims=True))
        a = (p * (1.0 / jnp.sum(p, 0, keepdims=True))).astype(bf16)
        s["A"][i, :, h * R : (h + 1) * R] = a
        s["combT"][i, rows, :] = mm(s["vT"][i, rows, :], a)
    if want_out:
        return x + mm(s["combT"][i].astype(bf16).T, w[3])
    return None


def spread_heads(x, out):
    for h in range(H):
        out[h * R : (h + 1) * R, :] = x * head_mask(h)


def back_start(g, w3T, s, i):
    gc = mm(g, w3T[...]).astype(bf16)
    s["gcT"][i] = gc.T
    spread_heads(gc, s["gcs"].at[i])


def back_heads(s, i):
    for h in range(H):
        rows = slice(D * h, D * (h + 1))
        cols = slice(h * R, (h + 1) * R)
        ga = mm(s["v"][i] * head_mask(h), s["gcT"][i])
        drow = jnp.sum(s["gcT"][i, rows, :].astype(f32) * s["combT"][i, rows, :], 0, keepdims=True)
        d = (s["A"][i, :, cols].astype(f32) * (ga - drow)).astype(bf16)
        s["Dm"][:, cols] = d
        s["gqT"][rows, :] = (mm(s["kT"][i, rows, :], d) * C).astype(bf16)
    mine = slice(i * R, (i + 1) * R)
    s["gqkv"][mine, 2 * N : 3 * N] = mm(s["A"][i], s["gcs"][i]).astype(bf16)
    s["gqkv"][mine, N : 2 * N] = (mm(s["Dm"][...], s["qs"][i]) * C).astype(bf16)
    s["gqkv"][mine, 0:N] = s["gqT"][...].T


def back_input(g, wT, gain, s, i):
    gh = mm(s["gqkv"][i * R : (i + 1) * R, :], wT[...])
    normed = s["normed"][i]
    t = gh * gain
    return g.astype(f32) + s["inv"][i] * (
        t - jnp.mean(t, -1, keepdims=True) - normed * jnp.mean(t * normed, -1, keepdims=True)
    )


def saved_scratch():
    def square(kind):
        return pltpu.VMEM((2, R, N), kind)

    def heads():
        return pltpu.VMEM((2, H * R, N), bf16)

    return dict(
        normed=square(f32),
        inv=pltpu.VMEM((2, R, 1), f32),
        hiddenT=pltpu.VMEM((N, 2 * R), bf16),
        q=square(bf16),
        qT=square(bf16),
        k=square(bf16),
        kT=square(bf16),
        v=square(bf16),
        vT=square(bf16),
        A=pltpu.VMEM((2, R, H * R), bf16),
        combT=square(f32),
        gqkv=pltpu.VMEM((2 * R, 3 * N), bf16),
        gcT=square(bf16),
        gcs=heads(),
        qs=heads(),
    )


def shared_scratch():
    return dict(Dm=pltpu.VMEM((R, H * R), bf16), gqT=pltpu.VMEM((N, R), bf16))


def weight_scratch():
    return dict(w=pltpu.VMEM((4, N, N), bf16), wT=pltpu.VMEM((3 * N, N), bf16), w3T=pltpu.VMEM((N, N), bf16))


SUMS = {"inter": 4, "out": 1, "proj": 3}


def comm_scratch():
    dma = pltpu.SemaphoreType.DMA
    half = pltpu.VMEM((R // 2, N), bf16)
    far = pltpu.VMEM((2, NG, 16, N), bf16)
    near = pltpu.VMEM((2, NR, 2, 16, N), bf16)
    bufs = dict(
        frames=pltpu.VMEM((R, N), bf16),
        upstream=pltpu.VMEM((2, R, N), bf16),
        gains=pltpu.VMEM((2, N), f32),
        upper=pltpu.VMEM((2, R, N), bf16),
        top=pltpu.VMEM((2, R, N), bf16),
        swap=pltpu.VMEM((R, R), bf16),
        turn=pltpu.VMEM((R, R), bf16),
        gather=pltpu.VMEM((2, R, 2 * R), bf16),
        halo=half,
        tail=half,
        tail_in=half,
        a_out=far,
        a_in=far,
        b_out=near,
        b_in=near,
        rb_out=near,
        rb_in=near,
        ra_out=far,
        ra_in=far,
    )
    count = dict(inputs=5, halo=1, tail=1, a=2 * NG, b=2 * NR, rb=2 * NR, ra=2 * NG)
    for name, m in SUMS.items():
        bufs[name + "_pair"] = pltpu.VMEM((CORE, NG, m, 16, 128), bf16)
        bufs[name + "_pair_in"] = pltpu.VMEM((NG, m, 16, 128), bf16)
        bufs[name + "_xy"] = pltpu.VMEM((NG, m, 16, 128), bf16)
        bufs[name + "_xy_in"] = pltpu.VMEM((NG, m, 16, 128), bf16)
        bufs[name + "_z"] = pltpu.VMEM((Z, m, 16, 128), bf16)
        bufs[name + "_all"] = pltpu.VMEM((CORE, NG, m, 16, 128), bf16)
        for stage, n in dict(pair=1, xy=NG, z=Z, share=NG, last=1).items():
            count[name + "_" + stage] = n
    sems = {}
    for name, n in count.items():
        sems[name + "_send"] = dma((n,))
        sems[name + "_recv"] = dma((n,))
    return bufs, sems


def loop(lo, hi, f):
    def step(d, carry):
        f(d)
        return carry

    lax.fori_loop(lo, hi, step, 0)


def digits(index, *sizes):
    found = []
    for n in reversed(sizes):
        found.append(jnp.bitwise_and(index, n - 1))
        index = jnp.right_shift(index, n.bit_length() - 1)
    return found[::-1]


def selection(rows, cols, source):
    row = lax.broadcasted_iota(jnp.int32, (rows, cols), 0)
    col = lax.broadcasted_iota(jnp.int32, (rows, cols), 1)
    return jnp.where(source(row) == col, 1.0, 0.0).astype(bf16)


def kernel(n_seq, frames_hbm, upstream_hbm, w1_hbm, w2_hbm, gains_hbm, gf, gw1, gw2, gg, s1, s2, shared, wt1, wt2, b, sems):
    s1, s2 = dict(s1, **shared), dict(s2, **shared)
    me, dp = lax.axis_index("seq"), lax.axis_index("dp")
    g, r = lax.div(me, NR), lax.rem(me, NR)
    x, zh = lax.div(g, ZH), lax.rem(g, ZH)
    y, core = lax.div(r, CORE), lax.rem(r, CORE)
    xy, z = x * Y + y, zh * DP + dp
    right, left = lax.rem(me + 1, n_seq), lax.rem(me + n_seq - 1, n_seq)

    def at_far(p):
        return {"seq": p * NR + r}

    def at_near(p):
        return {"seq": g * NR + p}

    def at_xy(p):
        return {"seq": ((lax.div(p, Y) * ZH + zh) * Y + lax.rem(p, Y)) * CORE + core}

    def at_z(p):
        return {"seq": ((x * ZH + lax.div(p, DP)) * Y + y) * CORE + core, "dp": lax.rem(p, DP)}

    other_core = {"seq": me + 1 - 2 * core}

    inputs = [
        pltpu.make_async_copy(src, dst, sems["inputs_send"].at[i])
        for i, (src, dst) in enumerate(
            (
                (frames_hbm.at[0], b["frames"]),
                (w1_hbm, wt1["w"]),
                (gains_hbm, b["gains"]),
                (upstream_hbm.at[0], b["upstream"]),
                (w2_hbm, wt2["w"]),
            )
        )
    ]
    for c in inputs:
        c.start()

    barrier = pltpu.get_barrier_semaphore()

    def greet(device):
        pl.semaphore_signal(barrier, inc=1, device_id=device, device_id_type=MESH)

    loop(1, NG, lambda d: greet(at_far(lax.rem(g + d, NG))))
    loop(0, ZH, lambda d: greet(at_z(lax.rem(zh + d, ZH) * DP + 1 - dp)))
    loop(
        0,
        (X - 1) * (Y - 1),
        lambda d: greet(
            at_xy(lax.rem(x + 1 + lax.div(d, Y - 1), X) * Y + lax.rem(y + 1 + lax.rem(d, Y - 1), Y))
        ),
    )
    loop(1, NR, lambda d: greet(at_near(lax.rem(r + d, NR))))
    greet({"seq": right})
    greet({"seq": left})
    greetings = NG - 1 + ZH + (X - 1) * (Y - 1) + NR - 1 + 2

    def copy(name, d, src, dst, to):
        return pltpu.make_async_remote_copy(
            src_ref=src,
            dst_ref=dst,
            send_sem=sems[name + "_send"].at[d],
            recv_sem=sems[name + "_recv"].at[d],
            device_id=to,
            device_id_type=MESH,
        )

    class Exchange:
        started = []

        def __init__(self, name, n, mine, address, src, dst, first=0):
            self.n = n

            def out(d):
                peer = lax.rem(mine + d, n)
                return copy(name, first + d, src(peer), dst(mine), address(peer))

            def came(d):
                peer = lax.rem(mine + n - d, n)
                return copy(name, first + d, src(peer), dst(peer), address(peer))

            self.out, self.came = out, came

        def start(self):
            loop(1, self.n, lambda d: self.out(d).start())
            self.started.append(self)

        def wait_recv(self):
            loop(1, self.n, lambda d: self.came(d).wait_recv())

        def wait_send(self):
            loop(1, self.n, lambda d: self.out(d).wait_send())

    def far_exchange(name, i):
        out, into = b[name + "_out"], b[name + "_in"]
        return Exchange(name, NG, g, at_far, lambda p: out.at[i, p], lambda p: into.at[i, p], NG * i)

    def near_exchange(name, i):
        out, into = b[name + "_out"], b[name + "_in"]
        return Exchange(name, NR, r, at_near, lambda p: out.at[i, p], lambda p: into.at[i, p], NR * i)

    ex_a = [far_exchange("a", c) for c in range(2)]
    ex_b = [near_exchange("b", i) for i in range(2)]
    ex_rb = [near_exchange("rb", i) for i in range(2)]
    ex_ra = [far_exchange("ra", i) for i in range(2)]

    class Sum:
        def __init__(self, name):
            self.m = SUMS[name]
            pair, pair_in = b[name + "_pair"], b[name + "_pair_in"]
            every = b[name + "_all"]
            self.pair, self.pair_in, self.every = pair, pair_in, every
            self.xy, self.xy_in, self.z = b[name + "_xy"], b[name + "_xy_in"], b[name + "_z"]
            self.ex_pair = copy(name + "_pair", 0, pair.at[1 - core], pair_in, other_core)
            self.ex_xy = Exchange(
                name + "_xy", NG, xy, at_xy, lambda p: self.xy.at[p], lambda p: self.xy_in.at[p]
            )
            self.ex_z = Exchange(name + "_z", Z, z, at_z, lambda p: self.z.at[z], lambda p: self.z.at[p])
            self.ex_share = Exchange(
                name + "_share", NG, xy, at_xy, lambda p: every.at[core, xy], lambda p: every.at[core, p]
            )
            self.ex_last = copy(name + "_last", 0, every.at[core], every.at[core], other_core)
            self.ex_last_in = copy(name + "_last", 0, every.at[1 - core], every.at[1 - core], other_core)

        def put(self, j, matrix):
            matrix = matrix.astype(bf16)
            for k in range(CORE):
                for p in range(NG):
                    row, lane = k * 128 + p // 2 * 16, p % 2 * 128
                    self.pair[k, p, j] = matrix[row : row + 16, lane : lane + 128]

        def first(self):
            self.ex_pair.start()

        def second(self):
            self.ex_pair.wait_recv()
            total = self.pair[core].astype(f32) + self.pair_in[...].astype(f32)
            self.xy[...] = total.astype(bf16)
            self.ex_xy.start()
            self.xy_in[xy] = self.xy[xy]

        def third(self):
            self.ex_xy.wait_recv()
            total = self.xy_in[0].astype(f32)
            for p in range(1, NG):
                total += self.xy_in[p].astype(f32)
            self.z[z] = total.astype(bf16)
            self.ex_z.start()

        def fourth(self):
            self.ex_z.wait_recv()
            total = self.z[0].astype(f32)
            for p in range(1, Z):
                total += self.z[p].astype(f32)
            self.every[core, xy] = total.astype(bf16)
            self.ex_share.start()

        def fifth(self):
            self.ex_share.wait_recv()
            self.ex_last.start()

        def finish(self, out, first):
            self.ex_last_in.wait_recv()
            for k in range(CORE):
                for p in range(NG):
                    row, lane = k * 128 + p // 2 * 16, p % 2 * 128
                    for j in range(self.m):
                        out[first + j, row : row + 16, lane : lane + 128] = self.every[k, p, j]

        def wait_send(self):
            self.ex_pair.wait_send()
            self.ex_last.wait_send()

    sum_inter, sum_out, sum_proj = Sum("inter"), Sum("out"), Sum("proj")

    def spread(c, out):
        b["a_out"][c] = out.astype(bf16).reshape(NG, 16, N)
        ex_a[c].start()
        b["a_in"][c, g] = b["a_out"][c, g]

    for c in inputs[:3]:
        c.wait()
    g1, g2 = b["gains"][0:1], b["gains"][1:2]
    own = b["frames"][...].astype(f32)
    out0 = forward(own, wt1["w"], g1, s1, 0, True)

    pl.semaphore_wait(barrier, greetings)
    halo = copy("halo", 0, b["frames"].at[0 : R // 2], b["halo"], {"seq": left})
    halo.start()
    spread(0, out0)

    b["swap"][...] = selection(R, R, lambda i: (lambda u, v: v * 16 + u)(*digits(i, 16, 16)))
    for c in inputs[3:]:
        c.wait()
    for i in range(2):
        b["upper"][i] = mm(b["swap"][...], b["upstream"][i]).astype(bf16)

    halo.wait_recv()
    following = jnp.where(me < n_seq - 1, b["halo"][...].astype(f32), 0.0)
    spread(1, forward(jnp.concatenate([own[R // 2 :], following], 0), wt1["w"], g1, s1, 1, True))

    for wt in (wt2, wt1):
        for j in range(3):
            wt["wT"][j * N : (j + 1) * N, :] = wt["w"][j].T
        wt["w3T"][...] = wt["w"][3].T
    b["turn"][...] = selection(R, R, lambda i: (lambda u, c, v: (v * 2 + c) * 16 + u)(*digits(i, NG, 2, NR)))
    for c in range(2):
        b["gather"][c] = selection(
            R, 2 * R, lambda i: (lambda u, v, p: ((p * NG + u) * 2 + c) * NR + v)(*digits(i, NG, NR, 2))
        )
    for i in range(2):
        back_start(b["upper"][i], wt2["w3T"], s2, i)
        spread_heads(s1["q"][i], s1["qs"].at[i])

    for c in range(2):
        ex_a[c].wait_recv()
        moved = mm(b["swap"][...], b["a_in"][c].reshape(R, N)).astype(bf16).reshape(NR, 2, 16, N)
        for i in range(2):
            b["b_out"][i, :, c] = moved[:, i]
    for i in range(2):
        ex_b[i].start()
        b["b_in"][i, r] = b["b_out"][i, r]

    def turn(i):
        ex_rb[i].wait_recv()
        b["ra_out"][i] = mm(b["turn"][...], b["rb_in"][i].reshape(R, N)).astype(bf16).reshape(NG, 16, N)
        ex_ra[i].start()
        b["ra_in"][i, g] = b["ra_out"][i, g]

    for i in range(2):
        ex_b[i].wait_recv()
        forward(b["b_in"][i].reshape(R, N).astype(f32), wt2["w"], g2, s2, i, False)
        spread_heads(s2["q"][i], s2["qs"].at[i])
        if i == 1:
            turn(0)
        back_heads(s2, i)
        dx = back_input(b["upper"][i], wt2["wT"], g2, s2, i)
        b["rb_out"][i] = dx.astype(bf16).reshape(NR, 2, 16, N)
        ex_rb[i].start()
        b["rb_in"][i, r] = b["rb_out"][i, r]

    def output_weights(s, top):
        return mm(s["combT"][0].astype(bf16), top[0]) + mm(s["combT"][1].astype(bf16), top[1])

    sum_inter.put(3, output_weights(s2, b["upper"]))
    proj = mm(s2["hiddenT"][...], s2["gqkv"][...])
    for j in range(3):
        sum_inter.put(j, proj[:, j * N : (j + 1) * N])
    sum_inter.first()
    turn(1)
    sum_inter.second()

    for i in range(2):
        ex_ra[i].wait_recv()
    came = b["ra_in"][...].reshape(2 * R, N)
    for c in range(2):
        b["top"][c] = mm(b["gather"][c], came).astype(bf16)
    for c in (1, 0):
        back_start(b["top"][c], wt1["w3T"], s1, c)
        if c == 1:
            sum_out.put(0, output_weights(s1, b["top"]))
            sum_out.first()
        back_heads(s1, c)
        if c == 1:
            sum_inter.third()
            sum_out.second()
    proj = mm(s1["hiddenT"][...], s1["gqkv"][...])
    for j in range(3):
        sum_proj.put(j, proj[:, j * N : (j + 1) * N])
    sum_proj.first()
    dx1 = back_input(b["top"][1], wt1["wT"], g1, s1, 1)
    b["tail"][...] = dx1[R // 2 :].astype(bf16)
    tail = copy("tail", 0, b["tail"], b["tail_in"], {"seq": right})
    tail.start()
    sum_proj.second()
    dx0 = back_input(b["top"][0], wt1["wT"], g1, s1, 0)
    sum_inter.fourth()
    sum_out.third()
    sum_proj.third()
    sum_out.fourth()
    sum_inter.fifth()
    tail.wait_recv()
    carried = jnp.where(me > 0, b["tail_in"][...].astype(f32), 0.0)
    gf[0, 0 : R // 2] = (dx0[0 : R // 2] + carried).astype(bf16)
    gf[0, R // 2 :] = (dx0[R // 2 :] + dx1[0 : R // 2]).astype(bf16)
    sum_proj.fourth()
    sum_out.fifth()

    def gain_sum(l, w, gw):
        total = w[0].astype(f32) * gw[0].astype(f32)
        for j in range(1, 3):
            total += w[j].astype(f32) * gw[j].astype(f32)
        rows = jnp.broadcast_to(jnp.sum(total, -1, keepdims=True), (N, 128))
        gg[l : l + 1] = rows.T[0:1] / b["gains"][l : l + 1]

    sum_inter.finish(gw2, 0)
    gain_sum(1, wt2["w"], gw2)
    sum_proj.fifth()
    sum_out.finish(gw1, 3)
    sum_proj.finish(gw1, 0)
    gain_sum(0, wt1["w"], gw1)

    halo.wait_send()
    tail.wait_send()
    for s in (sum_inter, sum_out, sum_proj):
        s.wait_send()
    for ex in Exchange.started:
        ex.wait_send()


def widen(gf, gw1, gw2, gg, gf_out, gw1_out, gw2_out, gg_out):
    gw1_out[...] = gw1[...].astype(f32)
    gw2_out[...] = gw2[...].astype(f32)
    gf_out[...] = gf[...]
    gg_out[...] = gg[...]


def on_device(n_seq, frames, upstream, w1, w2, gains):
    vmem = pl.BlockSpec(memory_space=pltpu.VMEM)
    bufs, sems = comm_scratch()

    def shapes(kind):
        return [
            jax.ShapeDtypeStruct(frames.shape, bf16),
            jax.ShapeDtypeStruct(w1.shape, kind),
            jax.ShapeDtypeStruct(w2.shape, kind),
            jax.ShapeDtypeStruct(gains.shape, f32),
        ]

    found = pl.pallas_call(
        functools.partial(kernel, n_seq),
        in_specs=[pl.BlockSpec(memory_space=pl.ANY)] * 5,
        out_specs=[vmem] * 4,
        out_shape=shapes(bf16),
        scratch_shapes=[
            saved_scratch(),
            saved_scratch(),
            shared_scratch(),
            weight_scratch(),
            weight_scratch(),
            bufs,
            sems,
        ],
        compiler_params=pltpu.CompilerParams(
            collective_id=0, has_side_effects=True, vmem_limit_bytes=56 * 2**20
        ),
        name="block_backward",
    )(frames, upstream, w1, w2, gains)
    return pl.pallas_call(
        widen,
        in_specs=[vmem] * 4,
        out_specs=[vmem] * 4,
        out_shape=shapes(f32),
        compiler_params=pltpu.CompilerParams(vmem_limit_bytes=60 * 2**20),
        name="widen",
    )(*found)


def solution(mesh):
    placed = (P("dp", "seq", None), P("dp", "seq", None, None), P(), P(), P())
    return jax.shard_map(
        functools.partial(on_device, mesh.shape["seq"]),
        mesh=mesh,
        in_specs=placed,
        out_specs=(P("dp", "seq", None), P(), P(), P()),
        check_vma=False,
    )
```

```python
import functools

import jax
import jax.numpy as jnp
from jax import lax
from jax.experimental import pallas as pl
from jax.experimental.pallas import tpu as pltpu
from jax.sharding import PartitionSpec as P

MESH = pl.DeviceIdType.MESH
bf16, f32 = jnp.bfloat16, jnp.float32

H = 8
D = 32
N = 256
R = 256
NR = 8
NG = 16
X, ZH, Y, CORE = 4, 4, 4, 2
DP = 2
Z = ZH * DP
EPS = 1e-05
C = D**-0.5
LOG2E = 1.4426950408889634


def mm(a, b):
    return jnp.dot(a, b, preferred_element_type=f32)


def head_mask(h):
    lane = lax.broadcasted_iota(jnp.int32, (1, N), 1)
    return jnp.where((lane >= D * h) & (lane < D * (h + 1)), 1.0, 0.0).astype(bf16)


def forward(x, w, gain, s, i, want_out):
    cen = x - jnp.mean(x, -1, keepdims=True)
    inv = lax.rsqrt(jnp.mean(cen * cen, -1, keepdims=True) + EPS)
    normed = cen * inv
    s["normed"][i] = normed
    s["inv"][i] = inv
    hidden = (normed * gain).astype(bf16)
    s["hiddenT"][:, i * R : (i + 1) * R] = hidden.T
    q = mm(hidden, w[0])
    s["q"][i] = q.astype(bf16)
    s["qT"][i] = (q * (C * LOG2E)).astype(bf16).T
    k = mm(hidden, w[1]).astype(bf16)
    s["k"][i] = k
    s["kT"][i] = k.T
    v = mm(hidden, w[2]).astype(bf16)
    s["v"][i] = v
    s["vT"][i] = v.T
    for h in range(H):
        rows = slice(D * h, D * (h + 1))
        scores = mm(s["k"][i] * head_mask(h), s["qT"][i])
        p = jnp.exp2(scores - jnp.max(scores, 0, keepdims=True))
        a = (p * (1.0 / jnp.sum(p, 0, keepdims=True))).astype(bf16)
        s["A"][i, :, h * R : (h + 1) * R] = a
        s["combT"][i, rows, :] = mm(s["vT"][i, rows, :], a)
    if want_out:
        return x + mm(s["combT"][i].astype(bf16).T, w[3])
    return None


def spread_heads(x, out):
    for h in range(H):
        out[h * R : (h + 1) * R, :] = x * head_mask(h)


def back_start(g, w3T, s, i):
    gc = mm(g, w3T[...]).astype(bf16)
    s["gcT"][i] = gc.T
    spread_heads(gc, s["gcs"].at[i])


def back_heads(s, i):
    for h in range(H):
        rows = slice(D * h, D * (h + 1))
        cols = slice(h * R, (h + 1) * R)
        ga = mm(s["v"][i] * head_mask(h), s["gcT"][i])
        drow = jnp.sum(s["gcT"][i, rows, :].astype(f32) * s["combT"][i, rows, :], 0, keepdims=True)
        d = (s["A"][i, :, cols].astype(f32) * (ga - drow)).astype(bf16)
        s["Dm"][:, cols] = d
        s["gqT"][rows, :] = (mm(s["kT"][i, rows, :], d) * C).astype(bf16)
    mine = slice(i * R, (i + 1) * R)
    s["gqkv"][mine, 2 * N : 3 * N] = mm(s["A"][i], s["gcs"][i]).astype(bf16)
    s["gqkv"][mine, N : 2 * N] = (mm(s["Dm"][...], s["qs"][i]) * C).astype(bf16)
    s["gqkv"][mine, 0:N] = s["gqT"][...].T


def back_input(g, wT, gain, s, i):
    gh = mm(s["gqkv"][i * R : (i + 1) * R, :], wT[...])
    normed = s["normed"][i]
    t = gh * gain
    return g.astype(f32) + s["inv"][i] * (
        t - jnp.mean(t, -1, keepdims=True) - normed * jnp.mean(t * normed, -1, keepdims=True)
    )


def saved_scratch():
    def square(kind):
        return pltpu.VMEM((2, R, N), kind)

    def heads():
        return pltpu.VMEM((2, H * R, N), bf16)

    return dict(
        normed=square(f32),
        inv=pltpu.VMEM((2, R, 1), f32),
        hiddenT=pltpu.VMEM((N, 2 * R), bf16),
        q=square(bf16),
        qT=square(bf16),
        k=square(bf16),
        kT=square(bf16),
        v=square(bf16),
        vT=square(bf16),
        A=pltpu.VMEM((2, R, H * R), bf16),
        combT=square(f32),
        gqkv=pltpu.VMEM((2 * R, 3 * N), bf16),
        gcT=square(bf16),
        gcs=heads(),
        qs=heads(),
    )


def shared_scratch():
    return dict(Dm=pltpu.VMEM((R, H * R), bf16), gqT=pltpu.VMEM((N, R), bf16))


def weight_scratch():
    return dict(w=pltpu.VMEM((4, N, N), bf16), wT=pltpu.VMEM((3 * N, N), bf16), w3T=pltpu.VMEM((N, N), bf16))


SUMS = {"inter": 4, "out": 1, "proj": 3}


def comm_scratch():
    dma = pltpu.SemaphoreType.DMA
    half = pltpu.VMEM((R // 2, N), bf16)
    far = pltpu.VMEM((2, NG, 16, N), bf16)
    near = pltpu.VMEM((2, NR, 2, 16, N), bf16)
    bufs = dict(
        frames=pltpu.VMEM((R, N), bf16),
        upstream=pltpu.VMEM((2, R, N), bf16),
        gains=pltpu.VMEM((2, N), f32),
        upper=pltpu.VMEM((2, R, N), bf16),
        top=pltpu.VMEM((2, R, N), bf16),
        swap=pltpu.VMEM((R, R), bf16),
        turn=pltpu.VMEM((R, R), bf16),
        gather=pltpu.VMEM((2, R, 2 * R), bf16),
        halo=half,
        tail=half,
        tail_in=half,
        a_out=far,
        a_in=far,
        b_out=near,
        b_in=near,
        rb_out=near,
        rb_in=near,
        ra_out=far,
        ra_in=far,
    )
    count = dict(inputs=5, halo=1, tail=1, a=2 * NG, b=2 * NR, rb=2 * NR, ra=2 * NG)
    for name, m in SUMS.items():
        bufs[name + "_pair"] = pltpu.VMEM((CORE, NG, m, 16, 128), bf16)
        bufs[name + "_pair_in"] = pltpu.VMEM((NG, m, 16, 128), bf16)
        bufs[name + "_xy"] = pltpu.VMEM((NG, m, 16, 128), bf16)
        bufs[name + "_xy_in"] = pltpu.VMEM((NG, m, 16, 128), bf16)
        bufs[name + "_z"] = pltpu.VMEM((Z, m, 16, 128), bf16)
        bufs[name + "_all"] = pltpu.VMEM((CORE, NG, m, 16, 128), bf16)
        for stage, n in dict(pair=1, xy=NG, z=Z, share=NG, last=1).items():
            count[name + "_" + stage] = n
    sems = {}
    for name, n in count.items():
        sems[name + "_send"] = dma((n,))
        sems[name + "_recv"] = dma((n,))
    return bufs, sems


def loop(lo, hi, f):
    def step(d, carry):
        f(d)
        return carry

    lax.fori_loop(lo, hi, step, 0)


def digits(index, *sizes):
    found = []
    for n in reversed(sizes):
        found.append(jnp.bitwise_and(index, n - 1))
        index = jnp.right_shift(index, n.bit_length() - 1)
    return found[::-1]


def selection(rows, cols, source):
    row = lax.broadcasted_iota(jnp.int32, (rows, cols), 0)
    col = lax.broadcasted_iota(jnp.int32, (rows, cols), 1)
    return jnp.where(source(row) == col, 1.0, 0.0).astype(bf16)


def kernel(n_seq, frames_hbm, upstream_hbm, w1_hbm, w2_hbm, gains_hbm, gf, gw1, gw2, gg, s1, s2, shared, wt1, wt2, b, sems):
    s1, s2 = dict(s1, **shared), dict(s2, **shared)
    me, dp = lax.axis_index("seq"), lax.axis_index("dp")
    g, r = lax.div(me, NR), lax.rem(me, NR)
    x, zh = lax.div(g, ZH), lax.rem(g, ZH)
    y, core = lax.div(r, CORE), lax.rem(r, CORE)
    xy, z = x * Y + y, zh * DP + dp
    right, left = lax.rem(me + 1, n_seq), lax.rem(me + n_seq - 1, n_seq)

    def at_far(p):
        return {"seq": p * NR + r}

    def at_near(p):
        return {"seq": g * NR + p}

    def at_xy(p):
        return {"seq": ((lax.div(p, Y) * ZH + zh) * Y + lax.rem(p, Y)) * CORE + core}

    def at_z(p):
        return {"seq": ((x * ZH + lax.div(p, DP)) * Y + y) * CORE + core, "dp": lax.rem(p, DP)}

    other_core = {"seq": me + 1 - 2 * core}

    inputs = [
        pltpu.make_async_copy(src, dst, sems["inputs_send"].at[i])
        for i, (src, dst) in enumerate(
            (
                (frames_hbm.at[0], b["frames"]),
                (w1_hbm, wt1["w"]),
                (gains_hbm, b["gains"]),
                (upstream_hbm.at[0], b["upstream"]),
                (w2_hbm, wt2["w"]),
            )
        )
    ]
    for c in inputs:
        c.start()

    barrier = pltpu.get_barrier_semaphore()

    def greet(device):
        pl.semaphore_signal(barrier, inc=1, device_id=device, device_id_type=MESH)

    loop(1, NG, lambda d: greet(at_far(lax.rem(g + d, NG))))
    loop(0, ZH, lambda d: greet(at_z(lax.rem(zh + d, ZH) * DP + 1 - dp)))
    loop(
        0,
        (X - 1) * (Y - 1),
        lambda d: greet(
            at_xy(lax.rem(x + 1 + lax.div(d, Y - 1), X) * Y + lax.rem(y + 1 + lax.rem(d, Y - 1), Y))
        ),
    )
    loop(1, NR, lambda d: greet(at_near(lax.rem(r + d, NR))))
    greet({"seq": right})
    greet({"seq": left})
    greetings = NG - 1 + ZH + (X - 1) * (Y - 1) + NR - 1 + 2

    def copy(name, d, src, dst, to):
        return pltpu.make_async_remote_copy(
            src_ref=src,
            dst_ref=dst,
            send_sem=sems[name + "_send"].at[d],
            recv_sem=sems[name + "_recv"].at[d],
            device_id=to,
            device_id_type=MESH,
        )

    class Exchange:
        started = []

        def __init__(self, name, n, mine, address, src, dst, first=0):
            self.n = n

            def out(d):
                peer = lax.rem(mine + d, n)
                return copy(name, first + d, src(peer), dst(mine), address(peer))

            def came(d):
                peer = lax.rem(mine + n - d, n)
                return copy(name, first + d, src(peer), dst(peer), address(peer))

            self.out, self.came = out, came

        def start(self):
            loop(1, self.n, lambda d: self.out(d).start())
            self.started.append(self)

        def wait_recv(self):
            loop(1, self.n, lambda d: self.came(d).wait_recv())

        def wait_send(self):
            loop(1, self.n, lambda d: self.out(d).wait_send())

    class Single:
        def __init__(self, out, came):
            self.out, self.came = out, came

        def start(self):
            self.out.start()
            Exchange.started.append(self)

        def wait_recv(self):
            self.came.wait_recv()

        def wait_send(self):
            self.out.wait_send()

    def far_exchange(name, i):
        out, into = b[name + "_out"], b[name + "_in"]
        return Exchange(name, NG, g, at_far, lambda p: out.at[i, p], lambda p: into.at[i, p], NG * i)

    def near_exchange(name, i):
        out, into = b[name + "_out"], b[name + "_in"]
        return Exchange(name, NR, r, at_near, lambda p: out.at[i, p], lambda p: into.at[i, p], NR * i)

    ex_a = [far_exchange("a", c) for c in range(2)]
    ex_b = [near_exchange("b", i) for i in range(2)]
    ex_rb = [near_exchange("rb", i) for i in range(2)]
    ex_ra = [far_exchange("ra", i) for i in range(2)]

    class Sum:
        def __init__(self, name):
            self.m = SUMS[name]
            pair, pair_in = b[name + "_pair"], b[name + "_pair_in"]
            every = b[name + "_all"]
            self.pair, self.pair_in, self.every = pair, pair_in, every
            self.xy, self.xy_in, self.z = b[name + "_xy"], b[name + "_xy_in"], b[name + "_z"]
            pair_out = copy(name + "_pair", 0, pair.at[1 - core], pair_in, other_core)
            self.ex_pair = Single(pair_out, pair_out)
            self.ex_xy = Exchange(
                name + "_xy", NG, xy, at_xy, lambda p: self.xy.at[p], lambda p: self.xy_in.at[p]
            )
            self.ex_z = Exchange(name + "_z", Z, z, at_z, lambda p: self.z.at[z], lambda p: self.z.at[p])
            self.ex_share = Exchange(
                name + "_share", NG, xy, at_xy, lambda p: every.at[core, xy], lambda p: every.at[core, p]
            )
            self.ex_last = Single(
                copy(name + "_last", 0, every.at[core], every.at[core], other_core),
                copy(name + "_last", 0, every.at[1 - core], every.at[1 - core], other_core),
            )

        def put(self, j, matrix):
            matrix = matrix.astype(bf16)
            for k in range(CORE):
                for p in range(NG):
                    row, lane = k * 128 + p // 2 * 16, p % 2 * 128
                    self.pair[k, p, j] = matrix[row : row + 16, lane : lane + 128]

        def first(self):
            self.ex_pair.start()

        def second(self):
            self.ex_pair.wait_recv()
            total = self.pair[core].astype(f32) + self.pair_in[...].astype(f32)
            self.xy[...] = total.astype(bf16)
            self.ex_xy.start()
            self.xy_in[xy] = self.xy[xy]

        def third(self):
            self.ex_xy.wait_recv()
            total = self.xy_in[0].astype(f32)
            for p in range(1, NG):
                total += self.xy_in[p].astype(f32)
            self.z[z] = total.astype(bf16)
            self.ex_z.start()

        def fourth(self):
            self.ex_z.wait_recv()
            total = self.z[0].astype(f32)
            for p in range(1, Z):
                total += self.z[p].astype(f32)
            self.every[core, xy] = total.astype(bf16)
            self.ex_share.start()

        def fifth(self):
            self.ex_share.wait_recv()
            self.ex_last.start()

        def finish(self, out, first):
            self.ex_last.wait_recv()
            for k in range(CORE):
                for p in range(NG):
                    row, lane = k * 128 + p // 2 * 16, p % 2 * 128
                    for j in range(self.m):
                        out[first + j, row : row + 16, lane : lane + 128] = self.every[k, p, j]

    sum_inter, sum_out, sum_proj = Sum("inter"), Sum("out"), Sum("proj")

    def spread(c, out):
        b["a_out"][c] = out.astype(bf16).reshape(NG, 16, N)
        ex_a[c].start()
        b["a_in"][c, g] = b["a_out"][c, g]

    for c in inputs[:3]:
        c.wait()
    g1, g2 = b["gains"][0:1], b["gains"][1:2]
    own = b["frames"][...].astype(f32)
    out0 = forward(own, wt1["w"], g1, s1, 0, True)

    pl.semaphore_wait(barrier, greetings)
    halo = copy("halo", 0, b["frames"].at[0 : R // 2], b["halo"], {"seq": left})
    halo = Single(halo, halo)
    halo.start()
    spread(0, out0)

    b["swap"][...] = selection(R, R, lambda i: (lambda u, v: v * 16 + u)(*digits(i, 16, 16)))
    for c in inputs[3:]:
        c.wait()
    for i in range(2):
        b["upper"][i] = mm(b["swap"][...], b["upstream"][i]).astype(bf16)

    halo.wait_recv()
    following = jnp.where(me < n_seq - 1, b["halo"][...].astype(f32), 0.0)
    spread(1, forward(jnp.concatenate([own[R // 2 :], following], 0), wt1["w"], g1, s1, 1, True))

    for wt in (wt2, wt1):
        for j in range(3):
            wt["wT"][j * N : (j + 1) * N, :] = wt["w"][j].T
        wt["w3T"][...] = wt["w"][3].T
    b["turn"][...] = selection(R, R, lambda i: (lambda u, c, v: (v * 2 + c) * 16 + u)(*digits(i, NG, 2, NR)))
    for c in range(2):
        b["gather"][c] = selection(
            R, 2 * R, lambda i: (lambda u, v, p: ((p * NG + u) * 2 + c) * NR + v)(*digits(i, NG, NR, 2))
        )
    for i in range(2):
        back_start(b["upper"][i], wt2["w3T"], s2, i)
        spread_heads(s1["q"][i], s1["qs"].at[i])

    for c in range(2):
        ex_a[c].wait_recv()
        moved = mm(b["swap"][...], b["a_in"][c].reshape(R, N)).astype(bf16).reshape(NR, 2, 16, N)
        for i in range(2):
            b["b_out"][i, :, c] = moved[:, i]
    for i in range(2):
        ex_b[i].start()
        b["b_in"][i, r] = b["b_out"][i, r]

    def turn(i):
        ex_rb[i].wait_recv()
        b["ra_out"][i] = mm(b["turn"][...], b["rb_in"][i].reshape(R, N)).astype(bf16).reshape(NG, 16, N)
        ex_ra[i].start()
        b["ra_in"][i, g] = b["ra_out"][i, g]

    for i in range(2):
        ex_b[i].wait_recv()
        forward(b["b_in"][i].reshape(R, N).astype(f32), wt2["w"], g2, s2, i, False)
        spread_heads(s2["q"][i], s2["qs"].at[i])
        if i == 1:
            turn(0)
        back_heads(s2, i)
        dx = back_input(b["upper"][i], wt2["wT"], g2, s2, i)
        b["rb_out"][i] = dx.astype(bf16).reshape(NR, 2, 16, N)
        ex_rb[i].start()
        b["rb_in"][i, r] = b["rb_out"][i, r]

    def output_weights(s, top):
        return mm(s["combT"][0].astype(bf16), top[0]) + mm(s["combT"][1].astype(bf16), top[1])

    sum_inter.put(3, output_weights(s2, b["upper"]))
    proj = mm(s2["hiddenT"][...], s2["gqkv"][...])
    for j in range(3):
        sum_inter.put(j, proj[:, j * N : (j + 1) * N])
    sum_inter.first()
    turn(1)
    sum_inter.second()

    for i in range(2):
        ex_ra[i].wait_recv()
    came = b["ra_in"][...].reshape(2 * R, N)
    for c in range(2):
        b["top"][c] = mm(b["gather"][c], came).astype(bf16)
    for c in (1, 0):
        back_start(b["top"][c], wt1["w3T"], s1, c)
        if c == 1:
            sum_out.put(0, output_weights(s1, b["top"]))
            sum_out.first()
        back_heads(s1, c)
        if c == 1:
            sum_inter.third()
            sum_out.second()
    proj = mm(s1["hiddenT"][...], s1["gqkv"][...])
    for j in range(3):
        sum_proj.put(j, proj[:, j * N : (j + 1) * N])
    sum_proj.first()
    dx1 = back_input(b["top"][1], wt1["wT"], g1, s1, 1)
    b["tail"][...] = dx1[R // 2 :].astype(bf16)
    tail = copy("tail", 0, b["tail"], b["tail_in"], {"seq": right})
    tail = Single(tail, tail)
    tail.start()
    sum_proj.second()
    dx0 = back_input(b["top"][0], wt1["wT"], g1, s1, 0)
    sum_inter.fourth()
    sum_out.third()
    sum_proj.third()
    sum_out.fourth()
    sum_inter.fifth()
    tail.wait_recv()
    carried = jnp.where(me > 0, b["tail_in"][...].astype(f32), 0.0)
    gf[0, 0 : R // 2] = (dx0[0 : R // 2] + carried).astype(bf16)
    gf[0, R // 2 :] = (dx0[R // 2 :] + dx1[0 : R // 2]).astype(bf16)
    sum_proj.fourth()
    sum_out.fifth()

    def gain_sum(l, w, gw):
        total = w[0].astype(f32) * gw[0].astype(f32)
        for j in range(1, 3):
            total += w[j].astype(f32) * gw[j].astype(f32)
        rows = jnp.broadcast_to(jnp.sum(total, -1, keepdims=True), (N, 128))
        gg[l : l + 1] = rows.T[0:1] / b["gains"][l : l + 1]

    sum_inter.finish(gw2, 0)
    gain_sum(1, wt2["w"], gw2)
    sum_proj.fifth()
    sum_out.finish(gw1, 3)
    sum_proj.finish(gw1, 0)
    gain_sum(0, wt1["w"], gw1)

    for ex in Exchange.started:
        ex.wait_send()


def widen(gf, gw1, gw2, gg, gf_out, gw1_out, gw2_out, gg_out):
    gw1_out[...] = gw1[...].astype(f32)
    gw2_out[...] = gw2[...].astype(f32)
    gf_out[...] = gf[...]
    gg_out[...] = gg[...]


def on_device(n_seq, frames, upstream, w1, w2, gains):
    vmem = pl.BlockSpec(memory_space=pltpu.VMEM)
    bufs, sems = comm_scratch()

    def shapes(kind):
        return [
            jax.ShapeDtypeStruct(frames.shape, bf16),
            jax.ShapeDtypeStruct(w1.shape, kind),
            jax.ShapeDtypeStruct(w2.shape, kind),
            jax.ShapeDtypeStruct(gains.shape, f32),
        ]

    found = pl.pallas_call(
        functools.partial(kernel, n_seq),
        in_specs=[pl.BlockSpec(memory_space=pl.ANY)] * 5,
        out_specs=[vmem] * 4,
        out_shape=shapes(bf16),
        scratch_shapes=[
            saved_scratch(),
            saved_scratch(),
            shared_scratch(),
            weight_scratch(),
            weight_scratch(),
            bufs,
            sems,
        ],
        compiler_params=pltpu.CompilerParams(
            collective_id=0, has_side_effects=True, vmem_limit_bytes=56 * 2**20
        ),
        name="block_backward",
    )(frames, upstream, w1, w2, gains)
    return pl.pallas_call(
        widen,
        in_specs=[vmem] * 4,
        out_specs=[vmem] * 4,
        out_shape=shapes(f32),
        compiler_params=pltpu.CompilerParams(vmem_limit_bytes=60 * 2**20),
        name="widen",
    )(*found)


def solution(mesh):
    placed = (P("dp", "seq", None), P("dp", "seq", None, None), P(), P(), P())
    return jax.shard_map(
        functools.partial(on_device, mesh.shape["seq"]),
        mesh=mesh,
        in_specs=placed,
        out_specs=(P("dp", "seq", None), P(), P(), P()),
        check_vma=False,
    )
```

```python
import functools

import jax
import jax.numpy as jnp
from jax import lax
from jax.experimental import pallas as pl
from jax.experimental.pallas import tpu as pltpu
from jax.sharding import PartitionSpec as P

MESH = pl.DeviceIdType.MESH
bf16, f32 = jnp.bfloat16, jnp.float32

H = 8
D = 32
N = 256
R = 256
NR = 8
NG = 16
X, ZH, Y, CORE = 4, 4, 4, 2
DP = 2
Z = ZH * DP
EPS = 1e-05
C = D**-0.5
LOG2E = 1.4426950408889634


def mm(a, b):
    return jnp.dot(a, b, preferred_element_type=f32)


def head_mask(h):
    lane = lax.broadcasted_iota(jnp.int32, (1, N), 1)
    return jnp.where((lane >= D * h) & (lane < D * (h + 1)), 1.0, 0.0).astype(bf16)


def tdot(a, b):
    return lax.dot_general(a, b, (((0,), (0,)), ((), ())), preferred_element_type=f32)


def forward(x, w, gain, s, i, want_out):
    cen = x - jnp.mean(x, -1, keepdims=True)
    inv = lax.rsqrt(jnp.mean(cen * cen, -1, keepdims=True) + EPS)
    normed = cen * inv
    s["normed"][i] = normed
    s["inv"][i] = inv
    hidden = (normed * gain).astype(bf16)
    s["k"][i] = mm(hidden, w[1]).astype(bf16)
    q = mm(hidden, w[0])
    s["qT"][i] = (q * (C * LOG2E)).astype(bf16).T
    s["q"][i] = q.astype(bf16)
    s["vT"][i] = mm(hidden, w[2]).astype(bf16).T
    for h in range(H):
        rows = slice(D * h, D * (h + 1))
        scores = mm(s["k"][i, :, rows], s["qT"][i, rows, :])
        p = jnp.exp2(scores - jnp.max(scores, 0, keepdims=True))
        s["A"][i, :, h * R : (h + 1) * R] = (p * (1.0 / jnp.sum(p, 0, keepdims=True))).astype(bf16)
    for h in range(H):
        rows = slice(D * h, D * (h + 1))
        s["combT"][i, rows, :] = mm(s["vT"][i, rows, :], s["A"][i, :, h * R : (h + 1) * R])
    s["kT"][i] = s["k"][i].T
    s["hiddenT"][:, i * R : (i + 1) * R] = hidden.T
    if want_out:
        return x + mm(s["combT"][i].astype(bf16).T, w[3])
    return None


def spread_heads(x, out):
    for h in range(H):
        out[h * R : (h + 1) * R, :] = x * head_mask(h)


def back_start(g, w3T, s, i):
    gc = mm(g, w3T[...]).astype(bf16)
    s["gcT"][i] = gc.T
    spread_heads(gc, s["gcs"].at[i])


def back_heads(s, i):
    for h in range(H):
        rows = slice(D * h, D * (h + 1))
        cols = slice(h * R, (h + 1) * R)
        ga = tdot(s["vT"][i, rows, :], s["gcT"][i, rows, :])
        drow = jnp.sum(s["gcT"][i, rows, :].astype(f32) * s["combT"][i, rows, :], 0, keepdims=True)
        s["Dm"][:, cols] = (s["A"][i, :, cols].astype(f32) * (ga - drow)).astype(bf16)
    for h in range(H):
        rows = slice(D * h, D * (h + 1))
        cols = slice(h * R, (h + 1) * R)
        s["gqT"][rows, :] = (mm(s["kT"][i, rows, :], s["Dm"][:, cols]) * C).astype(bf16)
    mine = slice(i * R, (i + 1) * R)
    s["gqkv"][mine, 2 * N : 3 * N] = mm(s["A"][i], s["gcs"][i]).astype(bf16)
    s["gqkv"][mine, N : 2 * N] = (mm(s["Dm"][...], s["qs"][i]) * C).astype(bf16)
    s["gqkv"][mine, 0:N] = s["gqT"][...].T


def back_input(g, wT, gain, s, i):
    gh = mm(s["gqkv"][i * R : (i + 1) * R, :], wT[...])
    normed = s["normed"][i]
    t = gh * gain
    return g.astype(f32) + s["inv"][i] * (
        t - jnp.mean(t, -1, keepdims=True) - normed * jnp.mean(t * normed, -1, keepdims=True)
    )


def saved_scratch():
    def square(kind):
        return pltpu.VMEM((2, R, N), kind)

    def heads():
        return pltpu.VMEM((2, H * R, N), bf16)

    return dict(
        normed=square(f32),
        inv=pltpu.VMEM((2, R, 1), f32),
        hiddenT=pltpu.VMEM((N, 2 * R), bf16),
        q=square(bf16),
        qT=square(bf16),
        k=square(bf16),
        kT=square(bf16),
        vT=square(bf16),
        A=pltpu.VMEM((2, R, H * R), bf16),
        combT=square(f32),
        gqkv=pltpu.VMEM((2 * R, 3 * N), bf16),
        gcT=square(bf16),
        gcs=heads(),
        qs=heads(),
    )


def shared_scratch():
    return dict(Dm=pltpu.VMEM((R, H * R), bf16), gqT=pltpu.VMEM((N, R), bf16))


def weight_scratch():
    return dict(w=pltpu.VMEM((4, N, N), bf16), wT=pltpu.VMEM((3 * N, N), bf16), w3T=pltpu.VMEM((N, N), bf16))


SUMS = {"inter": 4, "out": 1, "proj": 3}


def comm_scratch():
    dma = pltpu.SemaphoreType.DMA
    half = pltpu.VMEM((R // 2, N), bf16)
    far = pltpu.VMEM((2, NG, 16, N), bf16)
    near = pltpu.VMEM((2, NR, 2, 16, N), bf16)
    bufs = dict(
        frames=pltpu.VMEM((R, N), bf16),
        upstream=pltpu.VMEM((2, R, N), bf16),
        gains=pltpu.VMEM((2, N), f32),
        upper=pltpu.VMEM((2, R, N), bf16),
        top=pltpu.VMEM((2, R, N), bf16),
        swap=pltpu.VMEM((R, R), bf16),
        turn=pltpu.VMEM((R, R), bf16),
        gather=pltpu.VMEM((2, R, 2 * R), bf16),
        halo=half,
        tail=half,
        tail_in=half,
        a_out=far,
        a_in=far,
        b_out=near,
        b_in=near,
        rb_out=near,
        rb_in=near,
        ra_out=far,
        ra_in=far,
    )
    count = dict(inputs=5, halo=1, tail=1, a=2 * NG, b=2 * NR, rb=2 * NR, ra=2 * NG)
    for name, m in SUMS.items():
        bufs[name + "_pair"] = pltpu.VMEM((CORE, NG, m, 16, 128), bf16)
        bufs[name + "_pair_in"] = pltpu.VMEM((NG, m, 16, 128), bf16)
        bufs[name + "_xy"] = pltpu.VMEM((NG, m, 16, 128), bf16)
        bufs[name + "_xy_in"] = pltpu.VMEM((NG, m, 16, 128), bf16)
        bufs[name + "_z"] = pltpu.VMEM((Z, m, 16, 128), bf16)
        bufs[name + "_all"] = pltpu.VMEM((CORE, NG, m, 16, 128), bf16)
        for stage, n in dict(pair=1, xy=NG, z=Z, share=NG, last=1).items():
            count[name + "_" + stage] = n
    sems = {}
    for name, n in count.items():
        sems[name + "_send"] = dma((n,))
        sems[name + "_recv"] = dma((n,))
    return bufs, sems


def loop(lo, hi, f):
    def step(d, carry):
        f(d)
        return carry

    lax.fori_loop(lo, hi, step, 0)


def digits(index, *sizes):
    found = []
    for n in reversed(sizes):
        found.append(jnp.bitwise_and(index, n - 1))
        index = jnp.right_shift(index, n.bit_length() - 1)
    return found[::-1]


def selection(rows, cols, source):
    row = lax.broadcasted_iota(jnp.int32, (rows, cols), 0)
    col = lax.broadcasted_iota(jnp.int32, (rows, cols), 1)
    return jnp.where(source(row) == col, 1.0, 0.0).astype(bf16)


def kernel(n_seq, frames_hbm, upstream_hbm, w1_hbm, w2_hbm, gains_hbm, gf, gw1, gw2, gg, s1, s2, shared, wt1, wt2, b, sems):
    s1, s2 = dict(s1, **shared), dict(s2, **shared)
    me, dp = lax.axis_index("seq"), lax.axis_index("dp")
    g, r = lax.div(me, NR), lax.rem(me, NR)
    x, zh = lax.div(g, ZH), lax.rem(g, ZH)
    y, core = lax.div(r, CORE), lax.rem(r, CORE)
    xy, z = x * Y + y, zh * DP + dp
    right, left = lax.rem(me + 1, n_seq), lax.rem(me + n_seq - 1, n_seq)

    def at_far(p):
        return {"seq": p * NR + r}

    def at_near(p):
        return {"seq": g * NR + p}

    def at_xy(p):
        return {"seq": ((lax.div(p, Y) * ZH + zh) * Y + lax.rem(p, Y)) * CORE + core}

    def at_z(p):
        return {"seq": ((x * ZH + lax.div(p, DP)) * Y + y) * CORE + core, "dp": lax.rem(p, DP)}

    other_core = {"seq": me + 1 - 2 * core}

    inputs = [
        pltpu.make_async_copy(src, dst, sems["inputs_send"].at[i])
        for i, (src, dst) in enumerate(
            (
                (frames_hbm.at[0], b["frames"]),
                (w1_hbm, wt1["w"]),
                (gains_hbm, b["gains"]),
                (upstream_hbm.at[0], b["upstream"]),
                (w2_hbm, wt2["w"]),
            )
        )
    ]
    for c in inputs:
        c.start()

    barrier = pltpu.get_barrier_semaphore()

    def greet(device):
        pl.semaphore_signal(barrier, inc=1, device_id=device, device_id_type=MESH)

    loop(1, NG, lambda d: greet(at_far(lax.rem(g + d, NG))))
    loop(0, ZH, lambda d: greet(at_z(lax.rem(zh + d, ZH) * DP + 1 - dp)))
    loop(
        0,
        (X - 1) * (Y - 1),
        lambda d: greet(
            at_xy(lax.rem(x + 1 + lax.div(d, Y - 1), X) * Y + lax.rem(y + 1 + lax.rem(d, Y - 1), Y))
        ),
    )
    loop(1, NR, lambda d: greet(at_near(lax.rem(r + d, NR))))
    greet({"seq": right})
    greet({"seq": left})
    greetings = NG - 1 + ZH + (X - 1) * (Y - 1) + NR - 1 + 2

    def copy(name, d, src, dst, to):
        return pltpu.make_async_remote_copy(
            src_ref=src,
            dst_ref=dst,
            send_sem=sems[name + "_send"].at[d],
            recv_sem=sems[name + "_recv"].at[d],
            device_id=to,
            device_id_type=MESH,
        )

    class Exchange:
        started = []

        def __init__(self, name, n, mine, address, src, dst, first=0):
            self.n = n

            def out(d):
                peer = lax.rem(mine + d, n)
                return copy(name, first + d, src(peer), dst(mine), address(peer))

            def came(d):
                peer = lax.rem(mine + n - d, n)
                return copy(name, first + d, src(peer), dst(peer), address(peer))

            self.out, self.came = out, came

        def start(self):
            loop(1, self.n, lambda d: self.out(d).start())
            self.started.append(self)

        def wait_recv(self):
            loop(1, self.n, lambda d: self.came(d).wait_recv())

        def wait_send(self):
            loop(1, self.n, lambda d: self.out(d).wait_send())

    class Single:
        def __init__(self, out, came):
            self.out, self.came = out, came

        def start(self):
            self.out.start()
            Exchange.started.append(self)

        def wait_recv(self):
            self.came.wait_recv()

        def wait_send(self):
            self.out.wait_send()

    def far_exchange(name, i):
        out, into = b[name + "_out"], b[name + "_in"]
        return Exchange(name, NG, g, at_far, lambda p: out.at[i, p], lambda p: into.at[i, p], NG * i)

    def near_exchange(name, i):
        out, into = b[name + "_out"], b[name + "_in"]
        return Exchange(name, NR, r, at_near, lambda p: out.at[i, p], lambda p: into.at[i, p], NR * i)

    ex_a = [far_exchange("a", c) for c in range(2)]
    ex_b = [near_exchange("b", i) for i in range(2)]
    ex_rb = [near_exchange("rb", i) for i in range(2)]
    ex_ra = [far_exchange("ra", i) for i in range(2)]

    class Sum:
        def __init__(self, name):
            self.m = SUMS[name]
            pair, pair_in = b[name + "_pair"], b[name + "_pair_in"]
            every = b[name + "_all"]
            self.pair, self.pair_in, self.every = pair, pair_in, every
            self.xy, self.xy_in, self.z = b[name + "_xy"], b[name + "_xy_in"], b[name + "_z"]
            pair_out = copy(name + "_pair", 0, pair.at[1 - core], pair_in, other_core)
            self.ex_pair = Single(pair_out, pair_out)
            self.ex_xy = Exchange(
                name + "_xy", NG, xy, at_xy, lambda p: self.xy.at[p], lambda p: self.xy_in.at[p]
            )
            self.ex_z = Exchange(name + "_z", Z, z, at_z, lambda p: self.z.at[z], lambda p: self.z.at[p])
            self.ex_share = Exchange(
                name + "_share", NG, xy, at_xy, lambda p: every.at[core, xy], lambda p: every.at[core, p]
            )
            self.ex_last = Single(
                copy(name + "_last", 0, every.at[core], every.at[core], other_core),
                copy(name + "_last", 0, every.at[1 - core], every.at[1 - core], other_core),
            )

        def put(self, j, matrix):
            matrix = matrix.astype(bf16)
            for k in range(CORE):
                for p in range(NG):
                    row, lane = k * 128 + p // 2 * 16, p % 2 * 128
                    self.pair[k, p, j] = matrix[row : row + 16, lane : lane + 128]

        def first(self):
            self.ex_pair.start()

        def second(self):
            self.ex_pair.wait_recv()
            total = self.pair[core].astype(f32) + self.pair_in[...].astype(f32)
            self.xy[...] = total.astype(bf16)
            self.ex_xy.start()
            self.xy_in[xy] = self.xy[xy]

        def third(self):
            self.ex_xy.wait_recv()
            total = self.xy_in[0].astype(f32)
            for p in range(1, NG):
                total += self.xy_in[p].astype(f32)
            self.z[z] = total.astype(bf16)
            self.ex_z.start()

        def fourth(self):
            self.ex_z.wait_recv()
            total = self.z[0].astype(f32)
            for p in range(1, Z):
                total += self.z[p].astype(f32)
            self.every[core, xy] = total.astype(bf16)
            self.ex_share.start()

        def fifth(self):
            self.ex_share.wait_recv()
            self.ex_last.start()

        def finish(self, out, first):
            self.ex_last.wait_recv()
            for k in range(CORE):
                for p in range(NG):
                    row, lane = k * 128 + p // 2 * 16, p % 2 * 128
                    for j in range(self.m):
                        out[first + j, row : row + 16, lane : lane + 128] = self.every[k, p, j]

    sum_inter, sum_out, sum_proj = Sum("inter"), Sum("out"), Sum("proj")

    def spread(c, out):
        b["a_out"][c] = out.astype(bf16).reshape(NG, 16, N)
        ex_a[c].start()
        b["a_in"][c, g] = b["a_out"][c, g]

    for c in inputs[:3]:
        c.wait()
    g1, g2 = b["gains"][0:1], b["gains"][1:2]
    own = b["frames"][...].astype(f32)
    out0 = forward(own, wt1["w"], g1, s1, 0, True)

    pl.semaphore_wait(barrier, greetings)
    halo = copy("halo", 0, b["frames"].at[0 : R // 2], b["halo"], {"seq": left})
    halo = Single(halo, halo)
    halo.start()
    spread(0, out0)

    b["swap"][...] = selection(R, R, lambda i: (lambda u, v: v * 16 + u)(*digits(i, 16, 16)))
    for c in inputs[3:]:
        c.wait()
    for i in range(2):
        b["upper"][i] = mm(b["swap"][...], b["upstream"][i]).astype(bf16)

    halo.wait_recv()
    following = jnp.where(me < n_seq - 1, b["halo"][...].astype(f32), 0.0)
    spread(1, forward(jnp.concatenate([own[R // 2 :], following], 0), wt1["w"], g1, s1, 1, True))

    for wt in (wt2, wt1):
        for j in range(3):
            wt["wT"][j * N : (j + 1) * N, :] = wt["w"][j].T
        wt["w3T"][...] = wt["w"][3].T
    b["turn"][...] = selection(R, R, lambda i: (lambda u, c, v: (v * 2 + c) * 16 + u)(*digits(i, NG, 2, NR)))
    for c in range(2):
        b["gather"][c] = selection(
            R, 2 * R, lambda i: (lambda u, v, p: ((p * NG + u) * 2 + c) * NR + v)(*digits(i, NG, NR, 2))
        )
    for i in range(2):
        back_start(b["upper"][i], wt2["w3T"], s2, i)
        spread_heads(s1["q"][i], s1["qs"].at[i])

    for c in range(2):
        ex_a[c].wait_recv()
        moved = mm(b["swap"][...], b["a_in"][c].reshape(R, N)).astype(bf16).reshape(NR, 2, 16, N)
        for i in range(2):
            b["b_out"][i, :, c] = moved[:, i]
    for i in range(2):
        ex_b[i].start()
        b["b_in"][i, r] = b["b_out"][i, r]

    def turn(i):
        ex_rb[i].wait_recv()
        b["ra_out"][i] = mm(b["turn"][...], b["rb_in"][i].reshape(R, N)).astype(bf16).reshape(NG, 16, N)
        ex_ra[i].start()
        b["ra_in"][i, g] = b["ra_out"][i, g]

    for i in range(2):
        ex_b[i].wait_recv()
        forward(b["b_in"][i].reshape(R, N).astype(f32), wt2["w"], g2, s2, i, False)
        spread_heads(s2["q"][i], s2["qs"].at[i])
        if i == 1:
            turn(0)
        back_heads(s2, i)
        dx = back_input(b["upper"][i], wt2["wT"], g2, s2, i)
        b["rb_out"][i] = dx.astype(bf16).reshape(NR, 2, 16, N)
        ex_rb[i].start()
        b["rb_in"][i, r] = b["rb_out"][i, r]

    def output_weights(s, top):
        return mm(s["combT"][0].astype(bf16), top[0]) + mm(s["combT"][1].astype(bf16), top[1])

    sum_inter.put(3, output_weights(s2, b["upper"]))
    proj = mm(s2["hiddenT"][...], s2["gqkv"][...])
    for j in range(3):
        sum_inter.put(j, proj[:, j * N : (j + 1) * N])
    sum_inter.first()
    turn(1)
    sum_inter.second()

    for i in range(2):
        ex_ra[i].wait_recv()
    came = b["ra_in"][...].reshape(2 * R, N)
    for c in range(2):
        b["top"][c] = mm(b["gather"][c], came).astype(bf16)
    for c in (1, 0):
        back_start(b["top"][c], wt1["w3T"], s1, c)
        if c == 1:
            sum_out.put(0, output_weights(s1, b["top"]))
            sum_out.first()
        back_heads(s1, c)
        if c == 1:
            sum_inter.third()
            sum_out.second()
    proj = mm(s1["hiddenT"][...], s1["gqkv"][...])
    for j in range(3):
        sum_proj.put(j, proj[:, j * N : (j + 1) * N])
    sum_proj.first()
    dx1 = back_input(b["top"][1], wt1["wT"], g1, s1, 1)
    b["tail"][...] = dx1[R // 2 :].astype(bf16)
    tail = copy("tail", 0, b["tail"], b["tail_in"], {"seq": right})
    tail = Single(tail, tail)
    tail.start()
    sum_proj.second()
    dx0 = back_input(b["top"][0], wt1["wT"], g1, s1, 0)
    sum_inter.fourth()
    sum_out.third()
    sum_proj.third()
    sum_out.fourth()
    sum_inter.fifth()
    tail.wait_recv()
    carried = jnp.where(me > 0, b["tail_in"][...].astype(f32), 0.0)
    gf[0, 0 : R // 2] = (dx0[0 : R // 2] + carried).astype(bf16)
    gf[0, R // 2 :] = (dx0[R // 2 :] + dx1[0 : R // 2]).astype(bf16)
    sum_proj.fourth()
    sum_out.fifth()

    def gain_sum(l, w, gw):
        total = w[0].astype(f32) * gw[0].astype(f32)
        for j in range(1, 3):
            total += w[j].astype(f32) * gw[j].astype(f32)
        rows = jnp.broadcast_to(jnp.sum(total, -1, keepdims=True), (N, 128))
        gg[l : l + 1] = rows.T[0:1] / b["gains"][l : l + 1]

    sum_inter.finish(gw2, 0)
    gain_sum(1, wt2["w"], gw2)
    sum_proj.fifth()
    sum_out.finish(gw1, 3)
    sum_proj.finish(gw1, 0)
    gain_sum(0, wt1["w"], gw1)

    for ex in Exchange.started:
        ex.wait_send()


def widen(gf, gw1, gw2, gg, gf_out, gw1_out, gw2_out, gg_out):
    gw1_out[...] = gw1[...].astype(f32)
    gw2_out[...] = gw2[...].astype(f32)
    gf_out[...] = gf[...]
    gg_out[...] = gg[...]


def on_device(n_seq, frames, upstream, w1, w2, gains):
    vmem = pl.BlockSpec(memory_space=pltpu.VMEM)
    bufs, sems = comm_scratch()

    def shapes(kind):
        return [
            jax.ShapeDtypeStruct(frames.shape, bf16),
            jax.ShapeDtypeStruct(w1.shape, kind),
            jax.ShapeDtypeStruct(w2.shape, kind),
            jax.ShapeDtypeStruct(gains.shape, f32),
        ]

    found = pl.pallas_call(
        functools.partial(kernel, n_seq),
        in_specs=[pl.BlockSpec(memory_space=pl.ANY)] * 5,
        out_specs=[vmem] * 4,
        out_shape=shapes(bf16),
        scratch_shapes=[
            saved_scratch(),
            saved_scratch(),
            shared_scratch(),
            weight_scratch(),
            weight_scratch(),
            bufs,
            sems,
        ],
        compiler_params=pltpu.CompilerParams(
            collective_id=0, has_side_effects=True, vmem_limit_bytes=56 * 2**20
        ),
        name="block_backward",
    )(frames, upstream, w1, w2, gains)
    return pl.pallas_call(
        widen,
        in_specs=[vmem] * 4,
        out_specs=[vmem] * 4,
        out_shape=shapes(f32),
        compiler_params=pltpu.CompilerParams(vmem_limit_bytes=60 * 2**20),
        name="widen",
    )(*found)


def solution(mesh):
    placed = (P("dp", "seq", None), P("dp", "seq", None, None), P(), P(), P())
    return jax.shard_map(
        functools.partial(on_device, mesh.shape["seq"]),
        mesh=mesh,
        in_specs=placed,
        out_specs=(P("dp", "seq", None), P(), P(), P()),
        check_vma=False,
    )
```

```python
import functools

import jax
import jax.numpy as jnp
from jax import lax
from jax.experimental import pallas as pl
from jax.experimental.pallas import tpu as pltpu
from jax.sharding import PartitionSpec as P

MESH = pl.DeviceIdType.MESH
bf16, f32 = jnp.bfloat16, jnp.float32

H = 8
D = 32
N = 256
R = 256
NR = 8
NG = 16
X, ZH, Y, CORE = 4, 4, 4, 2
DP = 2
Z = ZH * DP
EPS = 1e-05
C = D**-0.5
LOG2E = 1.4426950408889634


def mm(a, b):
    return jnp.dot(a, b, preferred_element_type=f32)


def head_mask(h):
    lane = lax.broadcasted_iota(jnp.int32, (1, N), 1)
    return jnp.where((lane >= D * h) & (lane < D * (h + 1)), 1.0, 0.0).astype(bf16)


def tdot(a, b):
    return lax.dot_general(a, b, (((0,), (0,)), ((), ())), preferred_element_type=f32)


def forward(x, w, gain, s, i, want_out):
    cen = x - jnp.mean(x, -1, keepdims=True)
    inv = lax.rsqrt(jnp.mean(cen * cen, -1, keepdims=True) + EPS)
    normed = cen * inv
    s["normed"][i] = normed
    s["inv"][i] = inv
    hidden = (normed * gain).astype(bf16)
    s["k"][i] = mm(hidden, w[1]).astype(bf16)
    q = mm(hidden, w[0])
    s["qT"][i] = (q * (C * LOG2E)).astype(bf16).T
    s["q"][i] = q.astype(bf16)
    s["vT"][i] = mm(hidden, w[2]).astype(bf16).T
    for h in range(H):
        rows = slice(D * h, D * (h + 1))
        scores = mm(s["k"][i, :, rows], s["qT"][i, rows, :])
        p = jnp.exp2(scores - jnp.max(scores, 0, keepdims=True))
        s["A"][i, :, h * R : (h + 1) * R] = (p * (1.0 / jnp.sum(p, 0, keepdims=True))).astype(bf16)
    for h in range(H):
        rows = slice(D * h, D * (h + 1))
        s["combT"][i, rows, :] = mm(s["vT"][i, rows, :], s["A"][i, :, h * R : (h + 1) * R])
    s["kT"][i] = s["k"][i].T
    s["hiddenT"][:, i * R : (i + 1) * R] = hidden.T
    if want_out:
        return x + mm(s["combT"][i].astype(bf16).T, w[3])
    return None


def spread_heads(x, out):
    for h in range(H):
        out[h * R : (h + 1) * R, :] = x * head_mask(h)


def back_start(g, w3T, s, i):
    gc = mm(g, w3T[...]).astype(bf16)
    s["gcT"][i] = gc.T
    spread_heads(gc, s["gcs"].at[i])


def back_values(s, i):
    s["gqkv"][i * R : (i + 1) * R, 2 * N : 3 * N] = mm(s["A"][i], s["gcs"][i]).astype(bf16)


def back_heads(s, i):
    for h in range(H):
        rows = slice(D * h, D * (h + 1))
        cols = slice(h * R, (h + 1) * R)
        ga = tdot(s["vT"][i, rows, :], s["gcT"][i, rows, :])
        drow = jnp.sum(s["gcT"][i, rows, :].astype(f32) * s["combT"][i, rows, :], 0, keepdims=True)
        s["Dm"][:, cols] = (s["A"][i, :, cols].astype(f32) * (ga - drow)).astype(bf16)
    for h in range(H):
        rows = slice(D * h, D * (h + 1))
        cols = slice(h * R, (h + 1) * R)
        s["gqT"][rows, :] = (mm(s["kT"][i, rows, :], s["Dm"][:, cols]) * C).astype(bf16)
    mine = slice(i * R, (i + 1) * R)
    s["gqkv"][mine, N : 2 * N] = (mm(s["Dm"][...], s["qs"][i]) * C).astype(bf16)
    s["gqkv"][mine, 0:N] = s["gqT"][...].T


def back_input(g, wT, gain, s, i):
    gh = mm(s["gqkv"][i * R : (i + 1) * R, :], wT[...])
    normed = s["normed"][i]
    t = gh * gain
    return g.astype(f32) + s["inv"][i] * (
        t - jnp.mean(t, -1, keepdims=True) - normed * jnp.mean(t * normed, -1, keepdims=True)
    )


def saved_scratch():
    def square(kind):
        return pltpu.VMEM((2, R, N), kind)

    def heads():
        return pltpu.VMEM((2, H * R, N), bf16)

    return dict(
        normed=square(f32),
        inv=pltpu.VMEM((2, R, 1), f32),
        hiddenT=pltpu.VMEM((N, 2 * R), bf16),
        q=square(bf16),
        qT=square(bf16),
        k=square(bf16),
        kT=square(bf16),
        vT=square(bf16),
        A=pltpu.VMEM((2, R, H * R), bf16),
        combT=square(f32),
        gqkv=pltpu.VMEM((2 * R, 3 * N), bf16),
        gcT=square(bf16),
        gcs=heads(),
        qs=heads(),
    )


def shared_scratch():
    return dict(Dm=pltpu.VMEM((R, H * R), bf16), gqT=pltpu.VMEM((N, R), bf16))


def weight_scratch():
    return dict(w=pltpu.VMEM((4, N, N), bf16), wT=pltpu.VMEM((3 * N, N), bf16), w3T=pltpu.VMEM((N, N), bf16))


SUMS = {"inter": 4, "early": 2, "late": 2}


def comm_scratch():
    dma = pltpu.SemaphoreType.DMA
    half = pltpu.VMEM((R // 2, N), bf16)
    far = pltpu.VMEM((2, NG, 16, N), bf16)
    near = pltpu.VMEM((2, NR, 2, 16, N), bf16)
    bufs = dict(
        frames=pltpu.VMEM((R, N), bf16),
        upstream=pltpu.VMEM((2, R, N), bf16),
        gains=pltpu.VMEM((2, N), f32),
        upper=pltpu.VMEM((2, R, N), bf16),
        top=pltpu.VMEM((2, R, N), bf16),
        swap=pltpu.VMEM((R, R), bf16),
        turn=pltpu.VMEM((R, R), bf16),
        gather=pltpu.VMEM((2, R, 2 * R), bf16),
        halo=half,
        tail=half,
        tail_in=half,
        a_out=far,
        a_in=far,
        b_out=near,
        b_in=near,
        rb_out=near,
        rb_in=near,
        ra_out=far,
        ra_in=far,
    )
    count = dict(inputs=5, halo=1, tail=1, a=2 * NG, b=2 * NR, rb=2 * NR, ra=2 * NG)
    for name, m in SUMS.items():
        bufs[name + "_pair"] = pltpu.VMEM((CORE, NG, m, 16, 128), bf16)
        bufs[name + "_pair_in"] = pltpu.VMEM((NG, m, 16, 128), bf16)
        bufs[name + "_xy"] = pltpu.VMEM((NG, m, 16, 128), bf16)
        bufs[name + "_xy_in"] = pltpu.VMEM((NG, m, 16, 128), bf16)
        bufs[name + "_z"] = pltpu.VMEM((Z, m, 16, 128), bf16)
        bufs[name + "_all"] = pltpu.VMEM((CORE, NG, m, 16, 128), bf16)
        for stage, n in dict(pair=1, xy=NG, z=Z, share=NG, last=1).items():
            count[name + "_" + stage] = n
    sems = {}
    for name, n in count.items():
        sems[name + "_send"] = dma((n,))
        sems[name + "_recv"] = dma((n,))
    return bufs, sems


def digits(index, *sizes):
    found = []
    for n in reversed(sizes):
        found.append(jnp.bitwise_and(index, n - 1))
        index = jnp.right_shift(index, n.bit_length() - 1)
    return found[::-1]


def selection(rows, cols, source):
    row = lax.broadcasted_iota(jnp.int32, (rows, cols), 0)
    col = lax.broadcasted_iota(jnp.int32, (rows, cols), 1)
    return jnp.where(source(row) == col, 1.0, 0.0).astype(bf16)


def kernel(n_seq, frames_hbm, upstream_hbm, w1_hbm, w2_hbm, gains_hbm, gf, gw1, gw2, gg, s1, s2, shared, wt1, wt2, b, sems):
    s1, s2 = dict(s1, **shared), dict(s2, **shared)
    me, dp = lax.axis_index("seq"), lax.axis_index("dp")
    g, r = lax.div(me, NR), lax.rem(me, NR)
    x, zh = lax.div(g, ZH), lax.rem(g, ZH)
    y, core = lax.div(r, CORE), lax.rem(r, CORE)
    xy, z = x * Y + y, zh * DP + dp
    right, left = lax.rem(me + 1, n_seq), lax.rem(me + n_seq - 1, n_seq)

    def at_far(p):
        return {"seq": p * NR + r}

    def at_near(p):
        return {"seq": g * NR + p}

    def at_xy(p):
        return {"seq": ((lax.div(p, Y) * ZH + zh) * Y + lax.rem(p, Y)) * CORE + core}

    def at_z(p):
        return {"seq": ((x * ZH + lax.div(p, DP)) * Y + y) * CORE + core, "dp": lax.rem(p, DP)}

    other_core = {"seq": me + 1 - 2 * core}

    inputs = [
        pltpu.make_async_copy(src, dst, sems["inputs_send"].at[i])
        for i, (src, dst) in enumerate(
            (
                (frames_hbm.at[0], b["frames"]),
                (w1_hbm, wt1["w"]),
                (gains_hbm, b["gains"]),
                (upstream_hbm.at[0], b["upstream"]),
                (w2_hbm, wt2["w"]),
            )
        )
    ]
    for c in inputs:
        c.start()

    barrier = pltpu.get_barrier_semaphore()

    def greet(device):
        pl.semaphore_signal(barrier, inc=1, device_id=device, device_id_type=MESH)

    def ring(n):
        return lambda o: min(o, n - o)

    def pairs(first, n, second, m, weight):
        offsets = [(i, j) for i in range(n) for j in range(m) if i or j]
        offsets.sort(key=lambda o: -ring(n)(o[0]) - weight * ring(m)(o[1]))
        return [
            (
                lax.rem(first + i, n) * m + lax.rem(second + j, m),
                lax.rem(first + n - i, n) * m + lax.rem(second + m - j, m),
            )
            for i, j in offsets
        ]

    far_peers = pairs(x, X, zh, ZH, 2)
    near_peers = pairs(y, Y, core, CORE, 0.5)
    xy_peers = pairs(x, X, y, Y, 1)
    z_peers = [(lax.rem(z + o, Z), lax.rem(z + Z - o, Z)) for o in sorted(range(1, Z), key=lambda o: -ring(Z)(o))]

    greeted = [at_far(p) for p, _ in far_peers]
    greeted += [at_z(lax.rem(zh + o, ZH) * DP + 1 - dp) for o in (2, 1, 3, 0)]
    greeted += [
        at_xy(lax.rem(x + i, X) * Y + lax.rem(y + j, Y)) for i in (2, 1, 3) for j in (2, 1, 3)
    ]
    greeted += [at_near(p) for p, _ in near_peers] + [{"seq": right}, {"seq": left}]
    for device in greeted:
        greet(device)
    greetings = len(greeted)

    def copy(name, d, src, dst, to):
        return pltpu.make_async_remote_copy(
            src_ref=src,
            dst_ref=dst,
            send_sem=sems[name + "_send"].at[d],
            recv_sem=sems[name + "_recv"].at[d],
            device_id=to,
            device_id_type=MESH,
        )

    class Exchange:
        started = []

        def __init__(self, name, peers, mine, address, src, dst, first=0):
            self.out = [copy(name, first + i, src(to), dst(mine), address(to)) for i, (to, _) in enumerate(peers)]
            self.came = [copy(name, first + i, src(of), dst(of), address(of)) for i, (_, of) in enumerate(peers)]

        def start(self):
            for c in self.out:
                c.start()
            self.started.append(self)

        def wait_recv(self):
            for c in self.came:
                c.wait_recv()

        def wait_send(self):
            for c in self.out:
                c.wait_send()

    class Single:
        def __init__(self, out, came):
            self.out, self.came = out, came

        def start(self):
            self.out.start()
            Exchange.started.append(self)

        def wait_recv(self):
            self.came.wait_recv()

        def wait_send(self):
            self.out.wait_send()

    def far_exchange(name, i):
        out, into = b[name + "_out"], b[name + "_in"]
        return Exchange(name, far_peers, g, at_far, lambda p: out.at[i, p], lambda p: into.at[i, p], NG * i)

    def near_exchange(name, i):
        out, into = b[name + "_out"], b[name + "_in"]
        return Exchange(name, near_peers, r, at_near, lambda p: out.at[i, p], lambda p: into.at[i, p], NR * i)

    ex_a = [far_exchange("a", c) for c in range(2)]
    ex_b = [near_exchange("b", i) for i in range(2)]
    ex_rb = [near_exchange("rb", i) for i in range(2)]
    ex_ra = [far_exchange("ra", i) for i in range(2)]

    class Sum:
        def __init__(self, name):
            self.m = SUMS[name]
            pair, pair_in = b[name + "_pair"], b[name + "_pair_in"]
            every = b[name + "_all"]
            self.pair, self.pair_in, self.every = pair, pair_in, every
            self.xy, self.xy_in, self.z = b[name + "_xy"], b[name + "_xy_in"], b[name + "_z"]
            pair_out = copy(name + "_pair", 0, pair.at[1 - core], pair_in, other_core)
            self.ex_pair = Single(pair_out, pair_out)
            self.ex_xy = Exchange(
                name + "_xy", xy_peers, xy, at_xy, lambda p: self.xy.at[p], lambda p: self.xy_in.at[p]
            )
            self.ex_z = Exchange(name + "_z", z_peers, z, at_z, lambda p: self.z.at[z], lambda p: self.z.at[p])
            self.ex_share = Exchange(
                name + "_share", xy_peers, xy, at_xy, lambda p: every.at[core, xy], lambda p: every.at[core, p]
            )
            self.ex_last = Single(
                copy(name + "_last", 0, every.at[core], every.at[core], other_core),
                copy(name + "_last", 0, every.at[1 - core], every.at[1 - core], other_core),
            )

        def put(self, j, matrix):
            matrix = matrix.astype(bf16)
            for k in range(CORE):
                for p in range(NG):
                    row, lane = k * 128 + p // 2 * 16, p % 2 * 128
                    self.pair[k, p, j] = matrix[row : row + 16, lane : lane + 128]

        def first(self):
            self.ex_pair.start()

        def second(self):
            self.ex_pair.wait_recv()
            total = self.pair[core].astype(f32) + self.pair_in[...].astype(f32)
            self.xy[...] = total.astype(bf16)
            self.ex_xy.start()
            self.xy_in[xy] = self.xy[xy]

        def third(self):
            self.ex_xy.wait_recv()
            total = self.xy_in[0].astype(f32)
            for p in range(1, NG):
                total += self.xy_in[p].astype(f32)
            self.z[z] = total.astype(bf16)
            self.ex_z.start()

        def fourth(self):
            self.ex_z.wait_recv()
            total = self.z[0].astype(f32)
            for p in range(1, Z):
                total += self.z[p].astype(f32)
            self.every[core, xy] = total.astype(bf16)
            self.ex_share.start()

        def fifth(self):
            self.ex_share.wait_recv()
            self.ex_last.start()

        def finish(self, out, first):
            self.ex_last.wait_recv()
            for k in range(CORE):
                for p in range(NG):
                    row, lane = k * 128 + p // 2 * 16, p % 2 * 128
                    for j in range(self.m):
                        out[first + j, row : row + 16, lane : lane + 128] = self.every[k, p, j]

    sum_inter, sum_early, sum_late = Sum("inter"), Sum("early"), Sum("late")

    def spread(c, out):
        b["a_out"][c] = out.astype(bf16).reshape(NG, 16, N)
        ex_a[c].start()
        b["a_in"][c, g] = b["a_out"][c, g]

    for c in inputs[:3]:
        c.wait()
    g1, g2 = b["gains"][0:1], b["gains"][1:2]
    own = b["frames"][...].astype(f32)
    out0 = forward(own, wt1["w"], g1, s1, 0, True)

    pl.semaphore_wait(barrier, greetings)
    halo = copy("halo", 0, b["frames"].at[0 : R // 2], b["halo"], {"seq": left})
    halo = Single(halo, halo)
    halo.start()
    spread(0, out0)

    b["swap"][...] = selection(R, R, lambda i: (lambda u, v: v * 16 + u)(*digits(i, 16, 16)))
    for c in inputs[3:]:
        c.wait()
    for i in range(2):
        b["upper"][i] = mm(b["swap"][...], b["upstream"][i]).astype(bf16)

    halo.wait_recv()
    following = jnp.where(me < n_seq - 1, b["halo"][...].astype(f32), 0.0)
    spread(1, forward(jnp.concatenate([own[R // 2 :], following], 0), wt1["w"], g1, s1, 1, True))

    for wt in (wt2, wt1):
        for j in range(3):
            wt["wT"][j * N : (j + 1) * N, :] = wt["w"][j].T
        wt["w3T"][...] = wt["w"][3].T
    b["turn"][...] = selection(R, R, lambda i: (lambda u, c, v: (v * 2 + c) * 16 + u)(*digits(i, NG, 2, NR)))
    for c in range(2):
        b["gather"][c] = selection(
            R, 2 * R, lambda i: (lambda u, v, p: ((p * NG + u) * 2 + c) * NR + v)(*digits(i, NG, NR, 2))
        )
    for i in range(2):
        back_start(b["upper"][i], wt2["w3T"], s2, i)
        spread_heads(s1["q"][i], s1["qs"].at[i])

    for c in range(2):
        ex_a[c].wait_recv()
        moved = mm(b["swap"][...], b["a_in"][c].reshape(R, N)).astype(bf16).reshape(NR, 2, 16, N)
        for i in range(2):
            b["b_out"][i, :, c] = moved[:, i]
    for i in range(2):
        ex_b[i].start()
        b["b_in"][i, r] = b["b_out"][i, r]

    def turn(i):
        ex_rb[i].wait_recv()
        b["ra_out"][i] = mm(b["turn"][...], b["rb_in"][i].reshape(R, N)).astype(bf16).reshape(NG, 16, N)
        ex_ra[i].start()
        b["ra_in"][i, g] = b["ra_out"][i, g]

    for i in range(2):
        ex_b[i].wait_recv()
        forward(b["b_in"][i].reshape(R, N).astype(f32), wt2["w"], g2, s2, i, False)
        spread_heads(s2["q"][i], s2["qs"].at[i])
        if i == 1:
            turn(0)
        back_values(s2, i)
        back_heads(s2, i)
        dx = back_input(b["upper"][i], wt2["wT"], g2, s2, i)
        b["rb_out"][i] = dx.astype(bf16).reshape(NR, 2, 16, N)
        ex_rb[i].start()
        b["rb_in"][i, r] = b["rb_out"][i, r]

    def output_weights(s, top):
        return mm(s["combT"][0].astype(bf16), top[0]) + mm(s["combT"][1].astype(bf16), top[1])

    sum_inter.put(3, output_weights(s2, b["upper"]))
    proj = mm(s2["hiddenT"][...], s2["gqkv"][...])
    for j in range(3):
        sum_inter.put(j, proj[:, j * N : (j + 1) * N])
    sum_inter.first()
    sum_inter.second()
    turn(1)

    for i in range(2):
        ex_ra[i].wait_recv()
    came = b["ra_in"][...].reshape(2 * R, N)
    for c in range(2):
        b["top"][c] = mm(b["gather"][c], came).astype(bf16)
    for c in range(2):
        back_start(b["top"][c], wt1["w3T"], s1, c)
        back_values(s1, c)
    sum_early.put(0, mm(s1["hiddenT"][...], s1["gqkv"][:, 2 * N : 3 * N]))
    sum_early.put(1, output_weights(s1, b["top"]))
    sum_early.first()
    back_heads(s1, 1)
    sum_inter.third()
    sum_early.second()
    back_heads(s1, 0)
    proj = mm(s1["hiddenT"][...], s1["gqkv"][:, 0 : 2 * N])
    for j in range(2):
        sum_late.put(j, proj[:, j * N : (j + 1) * N])
    sum_late.first()
    dx1 = back_input(b["top"][1], wt1["wT"], g1, s1, 1)
    b["tail"][...] = dx1[R // 2 :].astype(bf16)
    tail = copy("tail", 0, b["tail"], b["tail_in"], {"seq": right})
    tail = Single(tail, tail)
    tail.start()
    sum_late.second()
    dx0 = back_input(b["top"][0], wt1["wT"], g1, s1, 0)
    sum_inter.fourth()
    sum_early.third()
    sum_late.third()
    sum_early.fourth()
    sum_inter.fifth()
    tail.wait_recv()
    carried = jnp.where(me > 0, b["tail_in"][...].astype(f32), 0.0)
    gf[0, 0 : R // 2] = (dx0[0 : R // 2] + carried).astype(bf16)
    gf[0, R // 2 :] = (dx0[R // 2 :] + dx1[0 : R // 2]).astype(bf16)
    sum_late.fourth()
    sum_early.fifth()

    def gain_sum(l, w, gw):
        total = w[0].astype(f32) * gw[0].astype(f32)
        for j in range(1, 3):
            total += w[j].astype(f32) * gw[j].astype(f32)
        rows = jnp.broadcast_to(jnp.sum(total, -1, keepdims=True), (N, 128))
        gg[l : l + 1] = rows.T[0:1] / b["gains"][l : l + 1]

    sum_inter.finish(gw2, 0)
    gain_sum(1, wt2["w"], gw2)
    sum_early.finish(gw1, 2)
    sum_late.fifth()
    sum_late.finish(gw1, 0)
    gain_sum(0, wt1["w"], gw1)

    for ex in Exchange.started:
        ex.wait_send()


def widen(gf, gw1, gw2, gg, gf_out, gw1_out, gw2_out, gg_out):
    gw1_out[...] = gw1[...].astype(f32)
    gw2_out[...] = gw2[...].astype(f32)
    gf_out[...] = gf[...]
    gg_out[...] = gg[...]


def on_device(n_seq, frames, upstream, w1, w2, gains):
    vmem = pl.BlockSpec(memory_space=pltpu.VMEM)
    bufs, sems = comm_scratch()

    def shapes(kind):
        return [
            jax.ShapeDtypeStruct(frames.shape, bf16),
            jax.ShapeDtypeStruct(w1.shape, kind),
            jax.ShapeDtypeStruct(w2.shape, kind),
            jax.ShapeDtypeStruct(gains.shape, f32),
        ]

    found = pl.pallas_call(
        functools.partial(kernel, n_seq),
        in_specs=[pl.BlockSpec(memory_space=pl.ANY)] * 5,
        out_specs=[vmem] * 4,
        out_shape=shapes(bf16),
        scratch_shapes=[
            saved_scratch(),
            saved_scratch(),
            shared_scratch(),
            weight_scratch(),
            weight_scratch(),
            bufs,
            sems,
        ],
        compiler_params=pltpu.CompilerParams(
            collective_id=0, has_side_effects=True, vmem_limit_bytes=56 * 2**20
        ),
        name="block_backward",
    )(frames, upstream, w1, w2, gains)
    step = [
        pl.BlockSpec((1, R // 4, N), lambda i: (0, i, 0)),
        pl.BlockSpec((1, N, N), lambda i: (i, 0, 0)),
        pl.BlockSpec((1, N, N), lambda i: (i, 0, 0)),
        pl.BlockSpec((2, N), lambda i: (0, 0)),
    ]
    return pl.pallas_call(
        widen,
        grid=(4,),
        in_specs=step,
        out_specs=step,
        out_shape=shapes(f32),
        compiler_params=pltpu.CompilerParams(vmem_limit_bytes=60 * 2**20),
        name="widen",
    )(*found)


def solution(mesh):
    placed = (P("dp", "seq", None), P("dp", "seq", None, None), P(), P(), P())
    return jax.shard_map(
        functools.partial(on_device, mesh.shape["seq"]),
        mesh=mesh,
        in_specs=placed,
        out_specs=(P("dp", "seq", None), P(), P(), P()),
        check_vma=False,
    )
```

```python
import functools

import jax
import jax.numpy as jnp
from jax import lax
from jax.experimental import pallas as pl
from jax.experimental.pallas import tpu as pltpu
from jax.sharding import PartitionSpec as P

MESH = pl.DeviceIdType.MESH
bf16, f32 = jnp.bfloat16, jnp.float32

H = 8
D = 32
N = 256
R = 256
NR = 8
NG = 16
X, ZH, Y, CORE = 4, 4, 4, 2
DP = 2
Z = ZH * DP
EPS = 1e-05
C = D**-0.5
LOG2E = 1.4426950408889634


def mm(a, b):
    return jnp.dot(a, b, preferred_element_type=f32)


def head_mask(h):
    lane = lax.broadcasted_iota(jnp.int32, (1, N), 1)
    return jnp.where((lane >= D * h) & (lane < D * (h + 1)), 1.0, 0.0).astype(bf16)


def tdot(a, b):
    return lax.dot_general(a, b, (((0,), (0,)), ((), ())), preferred_element_type=f32)


def forward(x, w, gain, s, i, want_out):
    cen = x - jnp.mean(x, -1, keepdims=True)
    inv = lax.rsqrt(jnp.mean(cen * cen, -1, keepdims=True) + EPS)
    normed = cen * inv
    s["normed"][i] = normed
    s["inv"][i] = inv
    hidden = (normed * gain).astype(bf16)
    s["k"][i] = mm(hidden, w[1]).astype(bf16)
    q = mm(hidden, w[0])
    s["qT"][i] = (q * (C * LOG2E)).astype(bf16).T
    s["q"][i] = q.astype(bf16)
    s["vT"][i] = mm(hidden, w[2]).astype(bf16).T
    for h in range(H):
        rows = slice(D * h, D * (h + 1))
        scores = mm(s["k"][i, :, rows], s["qT"][i, rows, :])
        p = jnp.exp2(scores - jnp.max(scores, 0, keepdims=True))
        s["A"][i, :, h * R : (h + 1) * R] = (p * (1.0 / jnp.sum(p, 0, keepdims=True))).astype(bf16)
    for h in range(H):
        rows = slice(D * h, D * (h + 1))
        s["combT"][i, rows, :] = mm(s["vT"][i, rows, :], s["A"][i, :, h * R : (h + 1) * R])
    s["kT"][i] = s["k"][i].T
    s["hiddenT"][:, i * R : (i + 1) * R] = hidden.T
    if want_out:
        return x + mm(s["combT"][i].astype(bf16).T, w[3])
    return None


def spread_heads(x, out):
    for h in range(H):
        out[h * R : (h + 1) * R, :] = x * head_mask(h)


def back_start(g, w3T, s, i):
    gc = mm(g, w3T[...]).astype(bf16)
    s["gcT"][i] = gc.T
    spread_heads(gc, s["gcs"].at[i])


def back_values(s, i):
    s["gqkv"][i * R : (i + 1) * R, 2 * N : 3 * N] = mm(s["A"][i], s["gcs"][i]).astype(bf16)


def back_heads(s, i):
    for h in range(H):
        rows = slice(D * h, D * (h + 1))
        cols = slice(h * R, (h + 1) * R)
        ga = tdot(s["vT"][i, rows, :], s["gcT"][i, rows, :])
        drow = jnp.sum(s["gcT"][i, rows, :].astype(f32) * s["combT"][i, rows, :], 0, keepdims=True)
        s["Dm"][:, cols] = (s["A"][i, :, cols].astype(f32) * (ga - drow)).astype(bf16)
    for h in range(H):
        rows = slice(D * h, D * (h + 1))
        cols = slice(h * R, (h + 1) * R)
        s["gqT"][rows, :] = (mm(s["kT"][i, rows, :], s["Dm"][:, cols]) * C).astype(bf16)
    mine = slice(i * R, (i + 1) * R)
    s["gqkv"][mine, N : 2 * N] = (mm(s["Dm"][...], s["qs"][i]) * C).astype(bf16)
    s["gqkv"][mine, 0:N] = s["gqT"][...].T


def back_input(g, wT, gain, s, i):
    gh = mm(s["gqkv"][i * R : (i + 1) * R, :], wT[...])
    normed = s["normed"][i]
    t = gh * gain
    return g.astype(f32) + s["inv"][i] * (
        t - jnp.mean(t, -1, keepdims=True) - normed * jnp.mean(t * normed, -1, keepdims=True)
    )


def saved_scratch():
    def square(kind):
        return pltpu.VMEM((2, R, N), kind)

    def heads():
        return pltpu.VMEM((2, H * R, N), bf16)

    return dict(
        normed=square(f32),
        inv=pltpu.VMEM((2, R, 1), f32),
        hiddenT=pltpu.VMEM((N, 2 * R), bf16),
        q=square(bf16),
        qT=square(bf16),
        k=square(bf16),
        kT=square(bf16),
        vT=square(bf16),
        A=pltpu.VMEM((2, R, H * R), bf16),
        combT=square(f32),
        gqkv=pltpu.VMEM((2 * R, 3 * N), bf16),
        gcT=square(bf16),
        gcs=heads(),
        qs=heads(),
    )


def shared_scratch():
    return dict(Dm=pltpu.VMEM((R, H * R), bf16), gqT=pltpu.VMEM((N, R), bf16))


def weight_scratch():
    return dict(w=pltpu.VMEM((4, N, N), bf16), wT=pltpu.VMEM((3 * N, N), bf16), w3T=pltpu.VMEM((N, N), bf16))


SUMS = {"inter": 4, "early": 2, "late": 2}


def comm_scratch():
    dma = pltpu.SemaphoreType.DMA
    half = pltpu.VMEM((R // 2, N), bf16)
    far = pltpu.VMEM((2, NG, 16, N), bf16)
    near = pltpu.VMEM((2, NR, 2, 16, N), bf16)
    bufs = dict(
        frames=pltpu.VMEM((R, N), bf16),
        upstream=pltpu.VMEM((2, R, N), bf16),
        gains=pltpu.VMEM((2, N), f32),
        upper=pltpu.VMEM((2, R, N), bf16),
        top=pltpu.VMEM((2, R, N), bf16),
        swap=pltpu.VMEM((R, R), bf16),
        turn=pltpu.VMEM((R, R), bf16),
        gather=pltpu.VMEM((2, R, 2 * R), bf16),
        halo=half,
        tail=half,
        tail_in=half,
        a_out=far,
        a_in=far,
        b_out=near,
        b_in=near,
        rb_out=near,
        rb_in=near,
        ra_out=far,
        ra_in=far,
    )
    count = dict(inputs=5, halo=1, tail=1, a=2 * NG, b=2 * NR, rb=2 * NR, ra=2 * NG)
    for name, m in SUMS.items():
        bufs[name + "_pair"] = pltpu.VMEM((CORE, NG, m, 16, 128), bf16)
        bufs[name + "_pair_in"] = pltpu.VMEM((NG, m, 16, 128), bf16)
        bufs[name + "_xy"] = pltpu.VMEM((NG, m, 16, 128), bf16)
        bufs[name + "_xy_in"] = pltpu.VMEM((NG, m, 16, 128), bf16)
        bufs[name + "_z"] = pltpu.VMEM((Z, m, 16, 128), bf16)
        bufs[name + "_all"] = pltpu.VMEM((CORE, NG, m, 16, 128), bf16)
        for stage, n in dict(pair=1, xy=NG, z=Z, share=NG, last=1).items():
            count[name + "_" + stage] = n
    sems = {}
    for name, n in count.items():
        sems[name + "_send"] = dma((n,))
        sems[name + "_recv"] = dma((n,))
    return bufs, sems


def digits(index, *sizes):
    found = []
    for n in reversed(sizes):
        found.append(jnp.bitwise_and(index, n - 1))
        index = jnp.right_shift(index, n.bit_length() - 1)
    return found[::-1]


def selection(rows, cols, source):
    row = lax.broadcasted_iota(jnp.int32, (rows, cols), 0)
    col = lax.broadcasted_iota(jnp.int32, (rows, cols), 1)
    return jnp.where(source(row) == col, 1.0, 0.0).astype(bf16)


def kernel(n_seq, frames_hbm, upstream_hbm, w1_hbm, w2_hbm, gains_hbm, gf, gw1, gw2, gg, s1, s2, shared, wt1, wt2, b, sems):
    s1, s2 = dict(s1, **shared), dict(s2, **shared)
    me, dp = lax.axis_index("seq"), lax.axis_index("dp")
    g, r = lax.div(me, NR), lax.rem(me, NR)
    x, zh = lax.div(g, ZH), lax.rem(g, ZH)
    y, core = lax.div(r, CORE), lax.rem(r, CORE)
    xy, z = x * Y + y, zh * DP + dp
    right, left = lax.rem(me + 1, n_seq), lax.rem(me + n_seq - 1, n_seq)

    def at_far(p):
        return {"seq": p * NR + r}

    def at_near(p):
        return {"seq": g * NR + p}

    def at_xy(p):
        return {"seq": ((lax.div(p, Y) * ZH + zh) * Y + lax.rem(p, Y)) * CORE + core}

    def at_z(p):
        return {"seq": ((x * ZH + lax.div(p, DP)) * Y + y) * CORE + core, "dp": lax.rem(p, DP)}

    other_core = {"seq": me + 1 - 2 * core}

    inputs = [
        pltpu.make_async_copy(src, dst, sems["inputs_send"].at[i])
        for i, (src, dst) in enumerate(
            (
                (frames_hbm.at[0], b["frames"]),
                (w1_hbm, wt1["w"]),
                (gains_hbm, b["gains"]),
                (upstream_hbm.at[0], b["upstream"]),
                (w2_hbm, wt2["w"]),
            )
        )
    ]
    for c in inputs:
        c.start()

    barrier = pltpu.get_barrier_semaphore()

    def greet(device):
        pl.semaphore_signal(barrier, inc=1, device_id=device, device_id_type=MESH)

    def ring(n):
        return lambda o: min(o, n - o)

    def pairs(first, n, second, m, weight):
        offsets = [(i, j) for i in range(n) for j in range(m) if i or j]
        offsets.sort(key=lambda o: -ring(n)(o[0]) - weight * ring(m)(o[1]))
        return [
            (
                lax.rem(first + i, n) * m + lax.rem(second + j, m),
                lax.rem(first + n - i, n) * m + lax.rem(second + m - j, m),
            )
            for i, j in offsets
        ]

    far_peers = pairs(x, X, zh, ZH, 2)
    near_peers = pairs(y, Y, core, CORE, 0.5)
    xy_peers = pairs(x, X, y, Y, 1)
    z_peers = [(lax.rem(z + o, Z), lax.rem(z + Z - o, Z)) for o in sorted(range(1, Z), key=lambda o: -ring(Z)(o))]

    greeted = [at_far(p) for p, _ in far_peers]
    greeted += [at_z(lax.rem(zh + o, ZH) * DP + 1 - dp) for o in (2, 1, 3, 0)]
    greeted += [
        at_xy(lax.rem(x + i, X) * Y + lax.rem(y + j, Y)) for i in (2, 1, 3) for j in (2, 1, 3)
    ]
    greeted += [at_near(p) for p, _ in near_peers] + [{"seq": right}, {"seq": left}]
    for device in greeted:
        greet(device)
    greetings = len(greeted)

    def copy(name, d, src, dst, to):
        return pltpu.make_async_remote_copy(
            src_ref=src,
            dst_ref=dst,
            send_sem=sems[name + "_send"].at[d],
            recv_sem=sems[name + "_recv"].at[d],
            device_id=to,
            device_id_type=MESH,
        )

    class Exchange:
        started = []

        def __init__(self, name, peers, mine, address, src, dst, first=0):
            self.out = [copy(name, first + i, src(to), dst(mine), address(to)) for i, (to, _) in enumerate(peers)]
            self.came = [copy(name, first + i, src(of), dst(of), address(of)) for i, (_, of) in enumerate(peers)]

        def start(self):
            for c in self.out:
                c.start()
            self.started.append(self)

        def wait_recv(self):
            for c in self.came:
                c.wait_recv()

        def wait_send(self):
            for c in self.out:
                c.wait_send()

    class Single:
        def __init__(self, out, came):
            self.out, self.came = out, came

        def start(self):
            self.out.start()
            Exchange.started.append(self)

        def wait_recv(self):
            self.came.wait_recv()

        def wait_send(self):
            self.out.wait_send()

    def far_exchange(name, i):
        out, into = b[name + "_out"], b[name + "_in"]
        return Exchange(name, far_peers, g, at_far, lambda p: out.at[i, p], lambda p: into.at[i, p], NG * i)

    def near_exchange(name, i):
        out, into = b[name + "_out"], b[name + "_in"]
        return Exchange(name, near_peers, r, at_near, lambda p: out.at[i, p], lambda p: into.at[i, p], NR * i)

    ex_a = [far_exchange("a", c) for c in range(2)]
    ex_b = [near_exchange("b", i) for i in range(2)]
    ex_rb = [near_exchange("rb", i) for i in range(2)]
    ex_ra = [far_exchange("ra", i) for i in range(2)]

    class Sum:
        def __init__(self, name):
            self.m = SUMS[name]
            pair, pair_in = b[name + "_pair"], b[name + "_pair_in"]
            every = b[name + "_all"]
            self.pair, self.pair_in, self.every = pair, pair_in, every
            self.xy, self.xy_in, self.z = b[name + "_xy"], b[name + "_xy_in"], b[name + "_z"]
            pair_out = copy(name + "_pair", 0, pair.at[1 - core], pair_in, other_core)
            self.ex_pair = Single(pair_out, pair_out)
            self.ex_xy = Exchange(
                name + "_xy", xy_peers, xy, at_xy, lambda p: self.xy.at[p], lambda p: self.xy_in.at[p]
            )
            self.ex_z = Exchange(name + "_z", z_peers, z, at_z, lambda p: self.z.at[z], lambda p: self.z.at[p])
            self.ex_share = Exchange(
                name + "_share", xy_peers, xy, at_xy, lambda p: every.at[core, xy], lambda p: every.at[core, p]
            )
            self.ex_last = Single(
                copy(name + "_last", 0, every.at[core], every.at[core], other_core),
                copy(name + "_last", 0, every.at[1 - core], every.at[1 - core], other_core),
            )

        def put(self, j, matrix):
            matrix = matrix.astype(bf16)
            for k in range(CORE):
                for p in range(NG):
                    row, lane = k * 128 + p // 2 * 16, p % 2 * 128
                    self.pair[k, p, j] = matrix[row : row + 16, lane : lane + 128]

        def first(self):
            self.ex_pair.start()

        def second(self):
            self.ex_pair.wait_recv()
            total = self.pair[core].astype(f32) + self.pair_in[...].astype(f32)
            self.xy[...] = total.astype(bf16)
            self.ex_xy.start()
            self.xy_in[xy] = self.xy[xy]

        def third(self):
            self.ex_xy.wait_recv()
            total = self.xy_in[0].astype(f32)
            for p in range(1, NG):
                total += self.xy_in[p].astype(f32)
            self.z[z] = total.astype(bf16)
            self.ex_z.start()

        def fourth(self):
            self.ex_z.wait_recv()
            total = self.z[0].astype(f32)
            for p in range(1, Z):
                total += self.z[p].astype(f32)
            self.every[core, xy] = total.astype(bf16)
            self.ex_share.start()

        def fifth(self):
            self.ex_share.wait_recv()
            self.ex_last.start()

        def finish(self, out, first):
            self.ex_last.wait_recv()
            for k in range(CORE):
                for p in range(NG):
                    row, lane = k * 128 + p // 2 * 16, p % 2 * 128
                    for j in range(self.m):
                        out[first + j, row : row + 16, lane : lane + 128] = self.every[k, p, j]

    sum_inter, sum_early, sum_late = Sum("inter"), Sum("early"), Sum("late")

    def spread(c, out):
        b["a_out"][c] = out.astype(bf16).reshape(NG, 16, N)
        ex_a[c].start()
        b["a_in"][c, g] = b["a_out"][c, g]

    for c in inputs[:3]:
        c.wait()
    g1, g2 = b["gains"][0:1], b["gains"][1:2]
    own = b["frames"][...].astype(f32)
    out0 = forward(own, wt1["w"], g1, s1, 0, True)

    pl.semaphore_wait(barrier, greetings)
    halo = copy("halo", 0, b["frames"].at[0 : R // 2], b["halo"], {"seq": left})
    halo = Single(halo, halo)
    halo.start()
    spread(0, out0)

    b["swap"][...] = selection(R, R, lambda i: (lambda u, v: v * 16 + u)(*digits(i, 16, 16)))
    for c in inputs[3:]:
        c.wait()
    for i in range(2):
        b["upper"][i] = mm(b["swap"][...], b["upstream"][i]).astype(bf16)

    halo.wait_recv()
    following = jnp.where(me < n_seq - 1, b["halo"][...].astype(f32), 0.0)
    spread(1, forward(jnp.concatenate([own[R // 2 :], following], 0), wt1["w"], g1, s1, 1, True))

    for wt in (wt2, wt1):
        for j in range(3):
            wt["wT"][j * N : (j + 1) * N, :] = wt["w"][j].T
        wt["w3T"][...] = wt["w"][3].T
    b["turn"][...] = selection(R, R, lambda i: (lambda u, c, v: (v * 2 + c) * 16 + u)(*digits(i, NG, 2, NR)))
    for c in range(2):
        b["gather"][c] = selection(
            R, 2 * R, lambda i: (lambda u, v, p: ((p * NG + u) * 2 + c) * NR + v)(*digits(i, NG, NR, 2))
        )
    for i in range(2):
        back_start(b["upper"][i], wt2["w3T"], s2, i)
        spread_heads(s1["q"][i], s1["qs"].at[i])

    for c in range(2):
        ex_a[c].wait_recv()
        moved = mm(b["swap"][...], b["a_in"][c].reshape(R, N)).astype(bf16).reshape(NR, 2, 16, N)
        for i in range(2):
            b["b_out"][i, :, c] = moved[:, i]
    for i in range(2):
        ex_b[i].start()
        b["b_in"][i, r] = b["b_out"][i, r]

    def turn(i):
        ex_rb[i].wait_recv()
        b["ra_out"][i] = mm(b["turn"][...], b["rb_in"][i].reshape(R, N)).astype(bf16).reshape(NG, 16, N)
        ex_ra[i].start()
        b["ra_in"][i, g] = b["ra_out"][i, g]

    for i in range(2):
        ex_b[i].wait_recv()
        forward(b["b_in"][i].reshape(R, N).astype(f32), wt2["w"], g2, s2, i, False)
        spread_heads(s2["q"][i], s2["qs"].at[i])
        back_values(s2, i)
        back_heads(s2, i)
        dx = back_input(b["upper"][i], wt2["wT"], g2, s2, i)
        b["rb_out"][i] = dx.astype(bf16).reshape(NR, 2, 16, N)
        ex_rb[i].start()
        b["rb_in"][i, r] = b["rb_out"][i, r]

    def output_weights(s, top):
        return mm(s["combT"][0].astype(bf16), top[0]) + mm(s["combT"][1].astype(bf16), top[1])

    sum_inter.put(3, output_weights(s2, b["upper"]))
    proj = mm(s2["hiddenT"][...], s2["gqkv"][...])
    for j in range(3):
        sum_inter.put(j, proj[:, j * N : (j + 1) * N])
    sum_inter.first()
    turn(0)
    sum_inter.second()
    turn(1)

    for i in range(2):
        ex_ra[i].wait_recv()
    came = b["ra_in"][...].reshape(2 * R, N)
    for c in range(2):
        b["top"][c] = mm(b["gather"][c], came).astype(bf16)
    for c in range(2):
        back_start(b["top"][c], wt1["w3T"], s1, c)
        back_values(s1, c)
    sum_early.put(0, mm(s1["hiddenT"][...], s1["gqkv"][:, 2 * N : 3 * N]))
    sum_early.put(1, output_weights(s1, b["top"]))
    sum_early.first()
    back_heads(s1, 1)
    sum_inter.third()
    sum_early.second()
    back_heads(s1, 0)
    proj = mm(s1["hiddenT"][...], s1["gqkv"][:, 0 : 2 * N])
    for j in range(2):
        sum_late.put(j, proj[:, j * N : (j + 1) * N])
    sum_late.first()
    dx1 = back_input(b["top"][1], wt1["wT"], g1, s1, 1)
    b["tail"][...] = dx1[R // 2 :].astype(bf16)
    tail = copy("tail", 0, b["tail"], b["tail_in"], {"seq": right})
    tail = Single(tail, tail)
    tail.start()
    sum_late.second()
    dx0 = back_input(b["top"][0], wt1["wT"], g1, s1, 0)
    sum_early.third()
    sum_late.third()
    sum_inter.fourth()
    sum_early.fourth()
    tail.wait_recv()
    carried = jnp.where(me > 0, b["tail_in"][...].astype(f32), 0.0)
    gf[0, 0 : R // 2] = (dx0[0 : R // 2] + carried).astype(bf16)
    gf[0, R // 2 :] = (dx0[R // 2 :] + dx1[0 : R // 2]).astype(bf16)
    sum_late.fourth()
    sum_inter.fifth()
    sum_early.fifth()

    def gain_sum(l, w, gw):
        total = w[0].astype(f32) * gw[0].astype(f32)
        for j in range(1, 3):
            total += w[j].astype(f32) * gw[j].astype(f32)
        rows = jnp.broadcast_to(jnp.sum(total, -1, keepdims=True), (N, 128))
        gg[l : l + 1] = rows.T[0:1] / b["gains"][l : l + 1]

    sum_inter.finish(gw2, 0)
    gain_sum(1, wt2["w"], gw2)
    sum_early.finish(gw1, 2)
    sum_late.fifth()
    sum_late.finish(gw1, 0)
    gain_sum(0, wt1["w"], gw1)

    for ex in Exchange.started:
        ex.wait_send()


def widen(gf, gw1, gw2, gg, gf_out, gw1_out, gw2_out, gg_out, narrow, wide, sems_in, sems_out, sems):
    whole = [pltpu.make_async_copy(gf, gf_out, sems.at[0]), pltpu.make_async_copy(gg, gg_out, sems.at[1])]
    blocks = [(l, j) for l in range(2) for j in range(4)]
    came = [pltpu.make_async_copy((gw1, gw2)[l].at[j], narrow.at[l, j], sems_in.at[l, j]) for l, j in blocks]
    gone = [pltpu.make_async_copy(wide.at[l, j], (gw1_out, gw2_out)[l].at[j], sems_out.at[l, j]) for l, j in blocks]
    for c in came + whole:
        c.start()
    for (l, j), into, out in zip(blocks, came, gone):
        into.wait()
        wide[l, j] = narrow[l, j].astype(f32)
        out.start()
    for c in gone + whole:
        c.wait()


def on_device(n_seq, frames, upstream, w1, w2, gains):
    vmem = pl.BlockSpec(memory_space=pltpu.VMEM)
    bufs, sems = comm_scratch()

    def shapes(kind):
        return [
            jax.ShapeDtypeStruct(frames.shape, bf16),
            jax.ShapeDtypeStruct(w1.shape, kind),
            jax.ShapeDtypeStruct(w2.shape, kind),
            jax.ShapeDtypeStruct(gains.shape, f32),
        ]

    found = pl.pallas_call(
        functools.partial(kernel, n_seq),
        in_specs=[pl.BlockSpec(memory_space=pl.ANY)] * 5,
        out_specs=[vmem] * 4,
        out_shape=shapes(bf16),
        scratch_shapes=[
            saved_scratch(),
            saved_scratch(),
            shared_scratch(),
            weight_scratch(),
            weight_scratch(),
            bufs,
            sems,
        ],
        compiler_params=pltpu.CompilerParams(
            collective_id=0, has_side_effects=True, vmem_limit_bytes=56 * 2**20
        ),
        name="block_backward",
    )(frames, upstream, w1, w2, gains)
    return pl.pallas_call(
        widen,
        in_specs=[pl.BlockSpec(memory_space=pl.ANY)] * 4,
        out_specs=[pl.BlockSpec(memory_space=pl.ANY)] * 4,
        out_shape=shapes(f32),
        scratch_shapes=[
            pltpu.VMEM((2, 4, N, N), bf16),
            pltpu.VMEM((2, 4, N, N), f32),
            pltpu.SemaphoreType.DMA((2, 4)),
            pltpu.SemaphoreType.DMA((2, 4)),
            pltpu.SemaphoreType.DMA((2,)),
        ],
        compiler_params=pltpu.CompilerParams(vmem_limit_bytes=60 * 2**20),
        name="widen",
    )(*found)


def solution(mesh):
    placed = (P("dp", "seq", None), P("dp", "seq", None, None), P(), P(), P())
    return jax.shard_map(
        functools.partial(on_device, mesh.shape["seq"]),
        mesh=mesh,
        in_specs=placed,
        out_specs=(P("dp", "seq", None), P(), P(), P()),
        check_vma=False,
    )
```

```python
import functools

import jax
import jax.numpy as jnp
from jax import lax
from jax.experimental import pallas as pl
from jax.experimental.pallas import tpu as pltpu
from jax.sharding import PartitionSpec as P

MESH = pl.DeviceIdType.MESH
bf16, f32 = jnp.bfloat16, jnp.float32

H = 8
D = 32
N = 256
R = 256
NR = 8
NG = 16
X, ZH, Y, CORE = 4, 4, 4, 2
DP = 2
Z = ZH * DP
EPS = 1e-05
C = D**-0.5
LOG2E = 1.4426950408889634


def mm(a, b):
    return jnp.dot(a, b, preferred_element_type=f32)


def head_mask(h):
    lane = lax.broadcasted_iota(jnp.int32, (1, N), 1)
    return jnp.where((lane >= D * h) & (lane < D * (h + 1)), 1.0, 0.0).astype(bf16)


def tdot(a, b):
    return lax.dot_general(a, b, (((0,), (0,)), ((), ())), preferred_element_type=f32)


def forward(x, w, gain, s, i, want_out):
    cen = x - jnp.mean(x, -1, keepdims=True)
    inv = lax.rsqrt(jnp.mean(cen * cen, -1, keepdims=True) + EPS)
    normed = cen * inv
    s["normed"][i] = normed
    s["inv"][i] = inv
    hidden = (normed * gain).astype(bf16)
    s["k"][i] = mm(hidden, w[1]).astype(bf16)
    q = mm(hidden, w[0])
    s["qT"][i] = (q * (C * LOG2E)).astype(bf16).T
    s["q"][i] = q.astype(bf16)
    s["vT"][i] = mm(hidden, w[2]).astype(bf16).T
    for h in range(H):
        rows = slice(D * h, D * (h + 1))
        scores = mm(s["k"][i, :, rows], s["qT"][i, rows, :])
        p = jnp.exp2(scores - jnp.max(scores, 0, keepdims=True))
        s["A"][i, :, h * R : (h + 1) * R] = (p * (1.0 / jnp.sum(p, 0, keepdims=True))).astype(bf16)
    for h in range(H):
        rows = slice(D * h, D * (h + 1))
        s["combT"][i, rows, :] = mm(s["vT"][i, rows, :], s["A"][i, :, h * R : (h + 1) * R])
    s["kT"][i] = s["k"][i].T
    s["hiddenT"][:, i * R : (i + 1) * R] = hidden.T
    if want_out:
        return x + mm(s["combT"][i].astype(bf16).T, w[3])
    return None


def spread_heads(x, out):
    for h in range(H):
        out[h * R : (h + 1) * R, :] = x * head_mask(h)


def back_start(g, w3T, s, i):
    gc = mm(g, w3T[...]).astype(bf16)
    s["gcT"][i] = gc.T
    spread_heads(gc, s["gcs"].at[i])


def back_values(s, i):
    s["gqkv"][i * R : (i + 1) * R, 2 * N : 3 * N] = mm(s["A"][i], s["gcs"][i]).astype(bf16)


def back_heads(s, i):
    for h in range(H):
        rows = slice(D * h, D * (h + 1))
        cols = slice(h * R, (h + 1) * R)
        ga = tdot(s["vT"][i, rows, :], s["gcT"][i, rows, :])
        drow = jnp.sum(s["gcT"][i, rows, :].astype(f32) * s["combT"][i, rows, :], 0, keepdims=True)
        s["Dm"][:, cols] = (s["A"][i, :, cols].astype(f32) * (ga - drow)).astype(bf16)
    for h in range(H):
        rows = slice(D * h, D * (h + 1))
        cols = slice(h * R, (h + 1) * R)
        s["gqT"][rows, :] = (mm(s["kT"][i, rows, :], s["Dm"][:, cols]) * C).astype(bf16)
    mine = slice(i * R, (i + 1) * R)
    s["gqkv"][mine, N : 2 * N] = (mm(s["Dm"][...], s["qs"][i]) * C).astype(bf16)
    s["gqkv"][mine, 0:N] = s["gqT"][...].T


def back_input(g, wT, gain, s, i):
    gh = mm(s["gqkv"][i * R : (i + 1) * R, :], wT[...])
    normed = s["normed"][i]
    t = gh * gain
    return g.astype(f32) + s["inv"][i] * (
        t - jnp.mean(t, -1, keepdims=True) - normed * jnp.mean(t * normed, -1, keepdims=True)
    )


def saved_scratch():
    def square(kind):
        return pltpu.VMEM((2, R, N), kind)

    def heads():
        return pltpu.VMEM((2, H * R, N), bf16)

    return dict(
        normed=square(f32),
        inv=pltpu.VMEM((2, R, 1), f32),
        hiddenT=pltpu.VMEM((N, 2 * R), bf16),
        q=square(bf16),
        qT=square(bf16),
        k=square(bf16),
        kT=square(bf16),
        vT=square(bf16),
        A=pltpu.VMEM((2, R, H * R), bf16),
        combT=square(f32),
        gqkv=pltpu.VMEM((2 * R, 3 * N), bf16),
        gcT=square(bf16),
        gcs=heads(),
        qs=heads(),
    )


def shared_scratch():
    return dict(Dm=pltpu.VMEM((R, H * R), bf16), gqT=pltpu.VMEM((N, R), bf16))


def weight_scratch():
    return dict(w=pltpu.VMEM((4, N, N), bf16), wT=pltpu.VMEM((3 * N, N), bf16), w3T=pltpu.VMEM((N, N), bf16))


SUMS = {"inter": 4, "early": 2, "late": 2}


def comm_scratch():
    dma = pltpu.SemaphoreType.DMA
    half = pltpu.VMEM((R // 2, N), bf16)
    far = pltpu.VMEM((2, NG, 16, N), bf16)
    near = pltpu.VMEM((2, NR, 2, 16, N), bf16)
    bufs = dict(
        frames=pltpu.VMEM((R, N), bf16),
        upstream=pltpu.VMEM((2, R, N), bf16),
        gains=pltpu.VMEM((2, N), f32),
        upper=pltpu.VMEM((2, R, N), bf16),
        top=pltpu.VMEM((2, R, N), bf16),
        swap=pltpu.VMEM((R, R), bf16),
        turn=pltpu.VMEM((R, R), bf16),
        gather=pltpu.VMEM((2, R, 2 * R), bf16),
        halo=half,
        tail=half,
        tail_in=half,
        a_out=far,
        a_in=far,
        b_out=near,
        b_in=near,
        rb_out=near,
        rb_in=near,
        ra_out=far,
        ra_in=far,
    )
    count = dict(inputs=5, halo=1, tail=1, a=2 * NG, b=2 * NR, rb=2 * NR, ra=2 * NG)
    for name, m in SUMS.items():
        bufs[name + "_pair"] = pltpu.VMEM((CORE, NG, m, 16, 128), bf16)
        bufs[name + "_pair_in"] = pltpu.VMEM((NG, m, 16, 128), bf16)
        bufs[name + "_xy"] = pltpu.VMEM((NG, m, 16, 128), bf16)
        bufs[name + "_xy_in"] = pltpu.VMEM((NG, m, 16, 128), bf16)
        bufs[name + "_z"] = pltpu.VMEM((Z, m, 16, 128), bf16)
        bufs[name + "_all"] = pltpu.VMEM((CORE, NG, m, 16, 128), bf16)
        for stage, n in dict(pair=1, xy=NG, z=Z, share=NG, last=1).items():
            count[name + "_" + stage] = n
    sems = {}
    for name, n in count.items():
        sems[name + "_send"] = dma((n,))
        sems[name + "_recv"] = dma((n,))
    return bufs, sems


def digits(index, *sizes):
    found = []
    for n in reversed(sizes):
        found.append(jnp.bitwise_and(index, n - 1))
        index = jnp.right_shift(index, n.bit_length() - 1)
    return found[::-1]


def selection(rows, cols, source):
    row = lax.broadcasted_iota(jnp.int32, (rows, cols), 0)
    col = lax.broadcasted_iota(jnp.int32, (rows, cols), 1)
    return jnp.where(source(row) == col, 1.0, 0.0).astype(bf16)


def kernel(n_seq, frames_hbm, upstream_hbm, w1_hbm, w2_hbm, gains_hbm, gf, gw1, gw2, gg, s1, s2, shared, wt1, wt2, b, sems):
    s1, s2 = dict(s1, **shared), dict(s2, **shared)
    me, dp = lax.axis_index("seq"), lax.axis_index("dp")
    g, r = lax.div(me, NR), lax.rem(me, NR)
    x, zh = lax.div(g, ZH), lax.rem(g, ZH)
    y, core = lax.div(r, CORE), lax.rem(r, CORE)
    xy, z = x * Y + y, zh * DP + dp
    right, left = lax.rem(me + 1, n_seq), lax.rem(me + n_seq - 1, n_seq)

    def at_far(p):
        return {"seq": p * NR + r}

    def at_near(p):
        return {"seq": g * NR + p}

    def at_xy(p):
        return {"seq": ((lax.div(p, Y) * ZH + zh) * Y + lax.rem(p, Y)) * CORE + core}

    def at_z(p):
        return {"seq": ((x * ZH + lax.div(p, DP)) * Y + y) * CORE + core, "dp": lax.rem(p, DP)}

    other_core = {"seq": me + 1 - 2 * core}

    inputs = [
        pltpu.make_async_copy(src, dst, sems["inputs_send"].at[i])
        for i, (src, dst) in enumerate(
            (
                (frames_hbm.at[0], b["frames"]),
                (w1_hbm, wt1["w"]),
                (gains_hbm, b["gains"]),
                (upstream_hbm.at[0], b["upstream"]),
                (w2_hbm, wt2["w"]),
            )
        )
    ]
    for c in inputs:
        c.start()

    barrier = pltpu.get_barrier_semaphore()

    def greet(device):
        pl.semaphore_signal(barrier, inc=1, device_id=device, device_id_type=MESH)

    def ring(n):
        return lambda o: min(o, n - o)

    def pairs(first, n, second, m, weight):
        offsets = [(i, j) for i in range(n) for j in range(m) if i or j]
        offsets.sort(key=lambda o: -ring(n)(o[0]) - weight * ring(m)(o[1]))
        return [
            (
                lax.rem(first + i, n) * m + lax.rem(second + j, m),
                lax.rem(first + n - i, n) * m + lax.rem(second + m - j, m),
            )
            for i, j in offsets
        ]

    far_peers = pairs(x, X, zh, ZH, 2)
    near_peers = pairs(y, Y, core, CORE, 0.5)
    xy_peers = pairs(x, X, y, Y, 1)
    z_peers = [(lax.rem(z + o, Z), lax.rem(z + Z - o, Z)) for o in sorted(range(1, Z), key=lambda o: -ring(Z)(o))]

    greeted = [at_far(p) for p, _ in far_peers]
    greeted += [at_z(lax.rem(zh + o, ZH) * DP + 1 - dp) for o in (2, 1, 3, 0)]
    greeted += [
        at_xy(lax.rem(x + i, X) * Y + lax.rem(y + j, Y)) for i in (2, 1, 3) for j in (2, 1, 3)
    ]
    greeted += [at_near(p) for p, _ in near_peers] + [{"seq": right}, {"seq": left}]
    for device in greeted:
        greet(device)
    greetings = len(greeted)

    def copy(name, d, src, dst, to):
        return pltpu.make_async_remote_copy(
            src_ref=src,
            dst_ref=dst,
            send_sem=sems[name + "_send"].at[d],
            recv_sem=sems[name + "_recv"].at[d],
            device_id=to,
            device_id_type=MESH,
        )

    class Exchange:
        started = []

        def __init__(self, name, peers, mine, address, src, dst, first=0):
            self.out = [copy(name, first + i, src(to), dst(mine), address(to)) for i, (to, _) in enumerate(peers)]
            self.came = [copy(name, first + i, src(of), dst(of), address(of)) for i, (_, of) in enumerate(peers)]

        def start(self):
            for c in self.out:
                c.start()
            self.started.append(self)

        def wait_recv(self):
            for c in self.came:
                c.wait_recv()

        def wait_send(self):
            for c in self.out:
                c.wait_send()

    class Single:
        def __init__(self, out, came):
            self.out, self.came = out, came

        def start(self):
            self.out.start()
            Exchange.started.append(self)

        def wait_recv(self):
            self.came.wait_recv()

        def wait_send(self):
            self.out.wait_send()

    def far_exchange(name, i):
        out, into = b[name + "_out"], b[name + "_in"]
        return Exchange(name, far_peers, g, at_far, lambda p: out.at[i, p], lambda p: into.at[i, p], NG * i)

    def near_exchange(name, i):
        out, into = b[name + "_out"], b[name + "_in"]
        return Exchange(name, near_peers, r, at_near, lambda p: out.at[i, p], lambda p: into.at[i, p], NR * i)

    ex_a = [far_exchange("a", c) for c in range(2)]
    ex_b = [near_exchange("b", i) for i in range(2)]
    ex_rb = [near_exchange("rb", i) for i in range(2)]
    ex_ra = [far_exchange("ra", i) for i in range(2)]

    class Sum:
        def __init__(self, name):
            self.m = SUMS[name]
            pair, pair_in = b[name + "_pair"], b[name + "_pair_in"]
            every = b[name + "_all"]
            self.pair, self.pair_in, self.every = pair, pair_in, every
            self.xy, self.xy_in, self.z = b[name + "_xy"], b[name + "_xy_in"], b[name + "_z"]
            pair_out = copy(name + "_pair", 0, pair.at[1 - core], pair_in, other_core)
            self.ex_pair = Single(pair_out, pair_out)
            self.ex_xy = Exchange(
                name + "_xy", xy_peers, xy, at_xy, lambda p: self.xy.at[p], lambda p: self.xy_in.at[p]
            )
            self.ex_z = Exchange(name + "_z", z_peers, z, at_z, lambda p: self.z.at[z], lambda p: self.z.at[p])
            self.ex_share = Exchange(
                name + "_share", xy_peers, xy, at_xy, lambda p: every.at[core, xy], lambda p: every.at[core, p]
            )
            self.ex_last = Single(
                copy(name + "_last", 0, every.at[core], every.at[core], other_core),
                copy(name + "_last", 0, every.at[1 - core], every.at[1 - core], other_core),
            )

        def put(self, j, matrix):
            matrix = matrix.astype(bf16)
            for k in range(CORE):
                for p in range(NG):
                    row, lane = k * 128 + p // 2 * 16, p % 2 * 128
                    self.pair[k, p, j] = matrix[row : row + 16, lane : lane + 128]

        def first(self):
            self.ex_pair.start()

        def second(self):
            self.ex_pair.wait_recv()
            total = self.pair[core].astype(f32) + self.pair_in[...].astype(f32)
            self.xy[...] = total.astype(bf16)
            self.ex_xy.start()
            self.xy_in[xy] = self.xy[xy]

        def third(self):
            self.ex_xy.wait_recv()
            total = self.xy_in[0].astype(f32)
            for p in range(1, NG):
                total += self.xy_in[p].astype(f32)
            self.z[z] = total.astype(bf16)
            self.ex_z.start()

        def fourth(self):
            self.ex_z.wait_recv()
            total = self.z[0].astype(f32)
            for p in range(1, Z):
                total += self.z[p].astype(f32)
            self.every[core, xy] = total.astype(bf16)
            self.ex_share.start()

        def fifth(self):
            self.ex_share.wait_recv()
            self.ex_last.start()

        def finish(self, out, first):
            self.ex_last.wait_recv()
            for k in range(CORE):
                for p in range(NG):
                    row, lane = k * 128 + p // 2 * 16, p % 2 * 128
                    for j in range(self.m):
                        out[first + j, row : row + 16, lane : lane + 128] = self.every[k, p, j]

    sum_inter, sum_early, sum_late = Sum("inter"), Sum("early"), Sum("late")

    def spread(c, out):
        b["a_out"][c] = out.astype(bf16).reshape(NG, 16, N)
        ex_a[c].start()
        b["a_in"][c, g] = b["a_out"][c, g]

    for c in inputs[:3]:
        c.wait()
    g1, g2 = b["gains"][0:1], b["gains"][1:2]
    own = b["frames"][...].astype(f32)
    out0 = forward(own, wt1["w"], g1, s1, 0, True)

    pl.semaphore_wait(barrier, greetings)
    halo = copy("halo", 0, b["frames"].at[0 : R // 2], b["halo"], {"seq": left})
    halo = Single(halo, halo)
    halo.start()
    spread(0, out0)

    b["swap"][...] = selection(R, R, lambda i: (lambda u, v: v * 16 + u)(*digits(i, 16, 16)))
    for c in inputs[3:]:
        c.wait()
    for i in range(2):
        b["upper"][i] = mm(b["swap"][...], b["upstream"][i]).astype(bf16)

    halo.wait_recv()
    following = jnp.where(me < n_seq - 1, b["halo"][...].astype(f32), 0.0)
    spread(1, forward(jnp.concatenate([own[R // 2 :], following], 0), wt1["w"], g1, s1, 1, True))

    for wt in (wt2, wt1):
        for j in range(3):
            wt["wT"][j * N : (j + 1) * N, :] = wt["w"][j].T
        wt["w3T"][...] = wt["w"][3].T
    b["turn"][...] = selection(R, R, lambda i: (lambda u, c, v: (v * 2 + c) * 16 + u)(*digits(i, NG, 2, NR)))
    for c in range(2):
        b["gather"][c] = selection(
            R, 2 * R, lambda i: (lambda u, v, p: ((p * NG + u) * 2 + c) * NR + v)(*digits(i, NG, NR, 2))
        )
    for i in range(2):
        back_start(b["upper"][i], wt2["w3T"], s2, i)
        spread_heads(s1["q"][i], s1["qs"].at[i])

    for c in range(2):
        ex_a[c].wait_recv()
        moved = mm(b["swap"][...], b["a_in"][c].reshape(R, N)).astype(bf16).reshape(NR, 2, 16, N)
        for i in range(2):
            b["b_out"][i, :, c] = moved[:, i]
    for i in range(2):
        ex_b[i].start()
        b["b_in"][i, r] = b["b_out"][i, r]

    def turn(i):
        ex_rb[i].wait_recv()
        b["ra_out"][i] = mm(b["turn"][...], b["rb_in"][i].reshape(R, N)).astype(bf16).reshape(NG, 16, N)
        ex_ra[i].start()
        b["ra_in"][i, g] = b["ra_out"][i, g]

    for i in range(2):
        ex_b[i].wait_recv()
        forward(b["b_in"][i].reshape(R, N).astype(f32), wt2["w"], g2, s2, i, False)
        spread_heads(s2["q"][i], s2["qs"].at[i])
        back_values(s2, i)
        back_heads(s2, i)
        dx = back_input(b["upper"][i], wt2["wT"], g2, s2, i)
        b["rb_out"][i] = dx.astype(bf16).reshape(NR, 2, 16, N)
        ex_rb[i].start()
        b["rb_in"][i, r] = b["rb_out"][i, r]

    def output_weights(s, top):
        return mm(s["combT"][0].astype(bf16), top[0]) + mm(s["combT"][1].astype(bf16), top[1])

    sum_inter.put(3, output_weights(s2, b["upper"]))
    proj = mm(s2["hiddenT"][...], s2["gqkv"][...])
    for j in range(3):
        sum_inter.put(j, proj[:, j * N : (j + 1) * N])
    sum_inter.first()
    turn(0)
    sum_inter.second()
    turn(1)

    for i in range(2):
        ex_ra[i].wait_recv()
    came = b["ra_in"][...].reshape(2 * R, N)
    for c in range(2):
        b["top"][c] = mm(b["gather"][c], came).astype(bf16)
    for c in range(2):
        back_start(b["top"][c], wt1["w3T"], s1, c)
        back_values(s1, c)
    sum_early.put(0, mm(s1["hiddenT"][...], s1["gqkv"][:, 2 * N : 3 * N]))
    sum_early.put(1, output_weights(s1, b["top"]))
    sum_early.first()
    back_heads(s1, 1)
    sum_inter.third()
    sum_early.second()
    back_heads(s1, 0)
    proj = mm(s1["hiddenT"][...], s1["gqkv"][:, 0 : 2 * N])
    for j in range(2):
        sum_late.put(j, proj[:, j * N : (j + 1) * N])
    sum_late.first()
    dx1 = back_input(b["top"][1], wt1["wT"], g1, s1, 1)
    b["tail"][...] = dx1[R // 2 :].astype(bf16)
    tail = copy("tail", 0, b["tail"], b["tail_in"], {"seq": right})
    tail = Single(tail, tail)
    tail.start()
    sum_late.second()
    dx0 = back_input(b["top"][0], wt1["wT"], g1, s1, 0)
    sum_early.third()
    sum_late.third()
    sum_inter.fourth()
    sum_early.fourth()
    tail.wait_recv()
    carried = jnp.where(me > 0, b["tail_in"][...].astype(f32), 0.0)
    gf[0, 0 : R // 2] = (dx0[0 : R // 2] + carried).astype(bf16)
    gf[0, R // 2 :] = (dx0[R // 2 :] + dx1[0 : R // 2]).astype(bf16)
    sum_late.fourth()
    sum_inter.fifth()
    sum_early.fifth()

    def gain_sum(l, w, gw):
        total = w[0].astype(f32) * gw[0].astype(f32)
        for j in range(1, 3):
            total += w[j].astype(f32) * gw[j].astype(f32)
        rows = jnp.broadcast_to(jnp.sum(total, -1, keepdims=True), (N, 128))
        gg[l : l + 1] = rows.T[0:1] / b["gains"][l : l + 1]

    sum_inter.finish(gw2, 0)
    gain_sum(1, wt2["w"], gw2)
    sum_early.finish(gw1, 2)
    sum_late.fifth()
    sum_late.finish(gw1, 0)
    gain_sum(0, wt1["w"], gw1)

    for ex in Exchange.started:
        ex.wait_send()


def widen(gf, gw1, gw2, gg, gf_out, gw1_out, gw2_out, gg_out):
    gw1_out[...] = gw1[...].astype(f32)
    gw2_out[...] = gw2[...].astype(f32)
    gf_out[...] = gf[...]
    gg_out[...] = gg[...]


def on_device(n_seq, frames, upstream, w1, w2, gains):
    vmem = pl.BlockSpec(memory_space=pltpu.VMEM)
    bufs, sems = comm_scratch()

    def shapes(kind):
        return [
            jax.ShapeDtypeStruct(frames.shape, bf16),
            jax.ShapeDtypeStruct(w1.shape, kind),
            jax.ShapeDtypeStruct(w2.shape, kind),
            jax.ShapeDtypeStruct(gains.shape, f32),
        ]

    found = pl.pallas_call(
        functools.partial(kernel, n_seq),
        in_specs=[pl.BlockSpec(memory_space=pl.ANY)] * 5,
        out_specs=[vmem] * 4,
        out_shape=shapes(bf16),
        scratch_shapes=[
            saved_scratch(),
            saved_scratch(),
            shared_scratch(),
            weight_scratch(),
            weight_scratch(),
            bufs,
            sems,
        ],
        compiler_params=pltpu.CompilerParams(
            collective_id=0, has_side_effects=True, vmem_limit_bytes=56 * 2**20
        ),
        name="block_backward",
    )(frames, upstream, w1, w2, gains)
    return pl.pallas_call(
        widen,
        in_specs=[vmem] * 4,
        out_specs=[vmem] * 4,
        out_shape=shapes(f32),
        compiler_params=pltpu.CompilerParams(vmem_limit_bytes=60 * 2**20),
        name="widen",
    )(*found)


def solution(mesh):
    placed = (P("dp", "seq", None), P("dp", "seq", None, None), P(), P(), P())
    return jax.shard_map(
        functools.partial(on_device, mesh.shape["seq"]),
        mesh=mesh,
        in_specs=placed,
        out_specs=(P("dp", "seq", None), P(), P(), P()),
        check_vma=False,
    )
```

```python
import functools

import jax
import jax.numpy as jnp
from jax import lax
from jax.experimental import pallas as pl
from jax.experimental.pallas import tpu as pltpu
from jax.sharding import PartitionSpec as P

MESH = pl.DeviceIdType.MESH
bf16, f32 = jnp.bfloat16, jnp.float32

H = 8
D = 32
N = 256
R = 256
NR = 8
NG = 16
X, ZH, Y, CORE = 4, 4, 4, 2
DP = 2
Z = ZH * DP
EPS = 1e-05
C = D**-0.5
LOG2E = 1.4426950408889634


def mm(a, b):
    return jnp.dot(a, b, preferred_element_type=f32)


def head_mask(h):
    lane = lax.broadcasted_iota(jnp.int32, (1, N), 1)
    return jnp.where((lane >= D * h) & (lane < D * (h + 1)), 1.0, 0.0).astype(bf16)


def tdot(a, b):
    return lax.dot_general(a, b, (((0,), (0,)), ((), ())), preferred_element_type=f32)


def forward(x, w, gain, s, i, want_out):
    cen = x - jnp.mean(x, -1, keepdims=True)
    inv = lax.rsqrt(jnp.mean(cen * cen, -1, keepdims=True) + EPS)
    normed = cen * inv
    s["normed"][i] = normed
    s["inv"][i] = inv
    hidden = (normed * gain).astype(bf16)
    s["k"][i] = mm(hidden, w[1]).astype(bf16)
    q = mm(hidden, w[0])
    s["qT"][i] = (q * (C * LOG2E)).astype(bf16).T
    s["q"][i] = q.astype(bf16)
    s["vT"][i] = mm(hidden, w[2]).astype(bf16).T
    for h in range(H):
        rows = slice(D * h, D * (h + 1))
        scores = mm(s["k"][i, :, rows], s["qT"][i, rows, :])
        p = jnp.exp2(scores - jnp.max(scores, 0, keepdims=True))
        s["A"][i, :, h * R : (h + 1) * R] = (p * (1.0 / jnp.sum(p, 0, keepdims=True))).astype(bf16)
    for h in range(H):
        rows = slice(D * h, D * (h + 1))
        s["combT"][i, rows, :] = mm(s["vT"][i, rows, :], s["A"][i, :, h * R : (h + 1) * R])
    s["kT"][i] = s["k"][i].T
    s["hiddenT"][:, i * R : (i + 1) * R] = hidden.T
    if want_out:
        return x + mm(s["combT"][i].astype(bf16).T, w[3])
    return None


def spread_heads(x, out):
    for h in range(H):
        out[h * R : (h + 1) * R, :] = x * head_mask(h)


def back_start(g, w3T, s, i):
    gc = mm(g, w3T[...]).astype(bf16)
    s["gcT"][i] = gc.T
    spread_heads(gc, s["gcs"].at[i])


def back_values(s, i):
    s["gqkv"][i * R : (i + 1) * R, 2 * N : 3 * N] = mm(s["A"][i], s["gcs"][i]).astype(bf16)


def back_heads(s, i):
    for h in range(H):
        rows = slice(D * h, D * (h + 1))
        cols = slice(h * R, (h + 1) * R)
        ga = tdot(s["vT"][i, rows, :], s["gcT"][i, rows, :])
        drow = jnp.sum(s["gcT"][i, rows, :].astype(f32) * s["combT"][i, rows, :], 0, keepdims=True)
        s["Dm"][:, cols] = (s["A"][i, :, cols].astype(f32) * (ga - drow)).astype(bf16)
    for h in range(H):
        rows = slice(D * h, D * (h + 1))
        cols = slice(h * R, (h + 1) * R)
        s["gqT"][rows, :] = (mm(s["kT"][i, rows, :], s["Dm"][:, cols]) * C).astype(bf16)
    mine = slice(i * R, (i + 1) * R)
    s["gqkv"][mine, N : 2 * N] = (mm(s["Dm"][...], s["qs"][i]) * C).astype(bf16)
    s["gqkv"][mine, 0:N] = s["gqT"][...].T


def back_input(g, wT, gain, s, i):
    gh = mm(s["gqkv"][i * R : (i + 1) * R, :], wT[...])
    normed = s["normed"][i]
    t = gh * gain
    return g.astype(f32) + s["inv"][i] * (
        t - jnp.mean(t, -1, keepdims=True) - normed * jnp.mean(t * normed, -1, keepdims=True)
    )


def saved_scratch():
    def square(kind):
        return pltpu.VMEM((2, R, N), kind)

    def heads():
        return pltpu.VMEM((2, H * R, N), bf16)

    return dict(
        normed=square(f32),
        inv=pltpu.VMEM((2, R, 1), f32),
        hiddenT=pltpu.VMEM((N, 2 * R), bf16),
        q=square(bf16),
        qT=square(bf16),
        k=square(bf16),
        kT=square(bf16),
        vT=square(bf16),
        A=pltpu.VMEM((2, R, H * R), bf16),
        combT=square(f32),
        gqkv=pltpu.VMEM((2 * R, 3 * N), bf16),
        gcT=square(bf16),
        gcs=heads(),
        qs=heads(),
    )


def shared_scratch():
    return dict(Dm=pltpu.VMEM((R, H * R), bf16), gqT=pltpu.VMEM((N, R), bf16))


def weight_scratch():
    return dict(w=pltpu.VMEM((4, N, N), bf16), wT=pltpu.VMEM((3 * N, N), bf16), w3T=pltpu.VMEM((N, N), bf16))


SUMS = {"inter": 4, "early": 2, "late": 2}


def comm_scratch():
    dma = pltpu.SemaphoreType.DMA
    half = pltpu.VMEM((R // 2, N), bf16)
    far = pltpu.VMEM((2, NG, 16, N), bf16)
    near = pltpu.VMEM((2, NR, 2, 16, N), bf16)
    bufs = dict(
        frames=pltpu.VMEM((R, N), bf16),
        upstream=pltpu.VMEM((2, R, N), bf16),
        gains=pltpu.VMEM((2, N), f32),
        upper=pltpu.VMEM((2, R, N), bf16),
        top=pltpu.VMEM((2, R, N), bf16),
        swap=pltpu.VMEM((R, R), bf16),
        turn=pltpu.VMEM((R, R), bf16),
        gather=pltpu.VMEM((2, R, 2 * R), bf16),
        halo=half,
        tail=half,
        tail_in=half,
        a_out=far,
        a_in=far,
        b_out=near,
        b_in=near,
        rb_out=near,
        rb_in=near,
        ra_out=far,
        ra_in=far,
    )
    count = dict(inputs=5, halo=1, tail=1, a=2 * NG, b=2 * NR, rb=2 * NR, ra=2 * NG)
    for name, m in SUMS.items():
        bufs[name + "_pair"] = pltpu.VMEM((CORE, NG, m, 16, 128), bf16)
        bufs[name + "_pair_in"] = pltpu.VMEM((NG, m, 16, 128), bf16)
        bufs[name + "_xy"] = pltpu.VMEM((NG, m, 16, 128), bf16)
        bufs[name + "_xy_in"] = pltpu.VMEM((NG, m, 16, 128), bf16)
        bufs[name + "_z"] = pltpu.VMEM((Z, m, 16, 128), bf16)
        bufs[name + "_all"] = pltpu.VMEM((CORE, NG, m, 16, 128), bf16)
        for stage, n in dict(pair=1, xy=NG, z=Z, share=NG, last=1).items():
            count[name + "_" + stage] = n
    sems = {}
    for name, n in count.items():
        sems[name + "_send"] = dma((n,))
        sems[name + "_recv"] = dma((n,))
    return bufs, sems


def digits(index, *sizes):
    found = []
    for n in reversed(sizes):
        found.append(jnp.bitwise_and(index, n - 1))
        index = jnp.right_shift(index, n.bit_length() - 1)
    return found[::-1]


def selection(rows, cols, source):
    row = lax.broadcasted_iota(jnp.int32, (rows, cols), 0)
    col = lax.broadcasted_iota(jnp.int32, (rows, cols), 1)
    return jnp.where(source(row) == col, 1.0, 0.0).astype(bf16)


def kernel(n_seq, frames_hbm, upstream_hbm, w1_hbm, w2_hbm, gains_hbm, gf, gw1, gw2, gg, s1, s2, shared, wt1, wt2, b, sems):
    s1, s2 = dict(s1, **shared), dict(s2, **shared)
    me, dp = lax.axis_index("seq"), lax.axis_index("dp")
    g, r = lax.div(me, NR), lax.rem(me, NR)
    x, zh = lax.div(g, ZH), lax.rem(g, ZH)
    y, core = lax.div(r, CORE), lax.rem(r, CORE)
    xy, z = x * Y + y, zh * DP + dp
    right, left = lax.rem(me + 1, n_seq), lax.rem(me + n_seq - 1, n_seq)

    def at_far(p):
        return {"seq": p * NR + r}

    def at_near(p):
        return {"seq": g * NR + p}

    def at_xy(p):
        return {"seq": ((lax.div(p, Y) * ZH + zh) * Y + lax.rem(p, Y)) * CORE + core}

    def at_z(p):
        return {"seq": ((x * ZH + lax.div(p, DP)) * Y + y) * CORE + core, "dp": lax.rem(p, DP)}

    other_core = {"seq": me + 1 - 2 * core}

    inputs = [
        pltpu.make_async_copy(src, dst, sems["inputs_send"].at[i])
        for i, (src, dst) in enumerate(
            (
                (frames_hbm.at[0], b["frames"]),
                (w1_hbm, wt1["w"]),
                (gains_hbm, b["gains"]),
                (upstream_hbm.at[0], b["upstream"]),
                (w2_hbm, wt2["w"]),
            )
        )
    ]
    for c in inputs:
        c.start()

    barrier = pltpu.get_barrier_semaphore()

    def greet(device):
        pl.semaphore_signal(barrier, inc=1, device_id=device, device_id_type=MESH)

    def ring(n):
        return lambda o: min(o, n - o)

    def pairs(first, n, second, m, weight):
        offsets = [(i, j) for i in range(n) for j in range(m) if i or j]
        offsets.sort(key=lambda o: -ring(n)(o[0]) - weight * ring(m)(o[1]))
        return [
            (
                lax.rem(first + i, n) * m + lax.rem(second + j, m),
                lax.rem(first + n - i, n) * m + lax.rem(second + m - j, m),
            )
            for i, j in offsets
        ]

    far_peers = pairs(x, X, zh, ZH, 2)
    near_peers = pairs(y, Y, core, CORE, 0.5)
    xy_peers = pairs(x, X, y, Y, 1)
    z_peers = [(lax.rem(z + o, Z), lax.rem(z + Z - o, Z)) for o in sorted(range(1, Z), key=lambda o: -ring(Z)(o))]

    greeted = [at_far(p) for p, _ in far_peers]
    greeted += [at_z(lax.rem(zh + o, ZH) * DP + 1 - dp) for o in (2, 1, 3, 0)]
    greeted += [
        at_xy(lax.rem(x + i, X) * Y + lax.rem(y + j, Y)) for i in (2, 1, 3) for j in (2, 1, 3)
    ]
    greeted += [at_near(p) for p, _ in near_peers] + [{"seq": right}, {"seq": left}]
    for device in greeted:
        greet(device)
    greetings = len(greeted)

    def copy(name, d, src, dst, to):
        return pltpu.make_async_remote_copy(
            src_ref=src,
            dst_ref=dst,
            send_sem=sems[name + "_send"].at[d],
            recv_sem=sems[name + "_recv"].at[d],
            device_id=to,
            device_id_type=MESH,
        )

    class Exchange:
        started = []

        def __init__(self, name, peers, mine, address, src, dst, first=0):
            self.out = [copy(name, first + i, src(to), dst(mine), address(to)) for i, (to, _) in enumerate(peers)]
            self.came = [copy(name, first + i, src(of), dst(of), address(of)) for i, (_, of) in enumerate(peers)]

        def start(self):
            for c in self.out:
                c.start()
            self.started.append(self)

        def wait_recv(self):
            for c in self.came:
                c.wait_recv()

        def wait_send(self):
            for c in self.out:
                c.wait_send()

    class Single:
        def __init__(self, out, came):
            self.out, self.came = out, came

        def start(self):
            self.out.start()
            Exchange.started.append(self)

        def wait_recv(self):
            self.came.wait_recv()

        def wait_send(self):
            self.out.wait_send()

    def far_exchange(name, i):
        out, into = b[name + "_out"], b[name + "_in"]
        return Exchange(name, far_peers, g, at_far, lambda p: out.at[i, p], lambda p: into.at[i, p], NG * i)

    def near_exchange(name, i):
        out, into = b[name + "_out"], b[name + "_in"]
        return Exchange(name, near_peers, r, at_near, lambda p: out.at[i, p], lambda p: into.at[i, p], NR * i)

    ex_a = [far_exchange("a", c) for c in range(2)]
    ex_b = [near_exchange("b", i) for i in range(2)]
    ex_rb = [near_exchange("rb", i) for i in range(2)]
    ex_ra = [far_exchange("ra", i) for i in range(2)]

    class Sum:
        def __init__(self, name):
            self.m = SUMS[name]
            pair, pair_in = b[name + "_pair"], b[name + "_pair_in"]
            every = b[name + "_all"]
            self.pair, self.pair_in, self.every = pair, pair_in, every
            self.xy, self.xy_in, self.z = b[name + "_xy"], b[name + "_xy_in"], b[name + "_z"]
            pair_out = copy(name + "_pair", 0, pair.at[1 - core], pair_in, other_core)
            self.ex_pair = Single(pair_out, pair_out)
            self.ex_xy = Exchange(
                name + "_xy", xy_peers, xy, at_xy, lambda p: self.xy.at[p], lambda p: self.xy_in.at[p]
            )
            self.ex_z = Exchange(name + "_z", z_peers, z, at_z, lambda p: self.z.at[z], lambda p: self.z.at[p])
            self.ex_share = Exchange(
                name + "_share", xy_peers, xy, at_xy, lambda p: every.at[core, xy], lambda p: every.at[core, p]
            )
            self.ex_last = Single(
                copy(name + "_last", 0, every.at[core], every.at[core], other_core),
                copy(name + "_last", 0, every.at[1 - core], every.at[1 - core], other_core),
            )

        def put(self, j, matrix):
            matrix = matrix.astype(bf16)
            for k in range(CORE):
                for p in range(NG):
                    row, lane = k * 128 + p // 2 * 16, p % 2 * 128
                    self.pair[k, p, j] = matrix[row : row + 16, lane : lane + 128]

        def first(self):
            self.ex_pair.start()

        def second(self):
            self.ex_pair.wait_recv()
            total = self.pair[core].astype(f32) + self.pair_in[...].astype(f32)
            self.xy[...] = total.astype(bf16)
            self.ex_xy.start()
            self.xy_in[xy] = self.xy[xy]

        def third(self):
            self.ex_xy.wait_recv()
            total = self.xy_in[0].astype(f32)
            for p in range(1, NG):
                total += self.xy_in[p].astype(f32)
            self.z[z] = total.astype(bf16)
            self.ex_z.start()

        def fourth(self):
            self.ex_z.wait_recv()
            total = self.z[0].astype(f32)
            for p in range(1, Z):
                total += self.z[p].astype(f32)
            self.every[core, xy] = total.astype(bf16)
            self.ex_share.start()

        def fifth(self):
            self.ex_share.wait_recv()
            self.ex_last.start()

        def finish(self, out, first):
            self.ex_last.wait_recv()
            for k in range(CORE):
                for p in range(NG):
                    row, lane = k * 128 + p // 2 * 16, p % 2 * 128
                    for j in range(self.m):
                        out[first + j, row : row + 16, lane : lane + 128] = self.every[k, p, j]

    sum_inter, sum_early, sum_late = Sum("inter"), Sum("early"), Sum("late")

    def spread(c, out):
        b["a_out"][c] = out.astype(bf16).reshape(NG, 16, N)
        ex_a[c].start()
        b["a_in"][c, g] = b["a_out"][c, g]

    for c in inputs[:3]:
        c.wait()
    g1, g2 = b["gains"][0:1], b["gains"][1:2]
    own = b["frames"][...].astype(f32)
    out0 = forward(own, wt1["w"], g1, s1, 0, True)

    pl.semaphore_wait(barrier, greetings)
    halo = copy("halo", 0, b["frames"].at[0 : R // 2], b["halo"], {"seq": left})
    halo = Single(halo, halo)
    halo.start()
    spread(0, out0)

    b["swap"][...] = selection(R, R, lambda i: (lambda u, v: v * 16 + u)(*digits(i, 16, 16)))
    for c in inputs[3:]:
        c.wait()
    for i in range(2):
        b["upper"][i] = mm(b["swap"][...], b["upstream"][i]).astype(bf16)

    halo.wait_recv()
    following = jnp.where(me < n_seq - 1, b["halo"][...].astype(f32), 0.0)
    spread(1, forward(jnp.concatenate([own[R // 2 :], following], 0), wt1["w"], g1, s1, 1, True))

    for wt in (wt2, wt1):
        for j in range(3):
            wt["wT"][j * N : (j + 1) * N, :] = wt["w"][j].T
        wt["w3T"][...] = wt["w"][3].T
    b["turn"][...] = selection(R, R, lambda i: (lambda u, c, v: (v * 2 + c) * 16 + u)(*digits(i, NG, 2, NR)))
    for c in range(2):
        b["gather"][c] = selection(
            R, 2 * R, lambda i: (lambda u, v, p: ((p * NG + u) * 2 + c) * NR + v)(*digits(i, NG, NR, 2))
        )
    for i in range(2):
        back_start(b["upper"][i], wt2["w3T"], s2, i)
        spread_heads(s1["q"][i], s1["qs"].at[i])

    for c in range(2):
        ex_a[c].wait_recv()
        moved = mm(b["swap"][...], b["a_in"][c].reshape(R, N)).astype(bf16).reshape(NR, 2, 16, N)
        for i in range(2):
            b["b_out"][i, :, c] = moved[:, i]
    for i in range(2):
        ex_b[i].start()
        b["b_in"][i, r] = b["b_out"][i, r]

    def turn(i):
        ex_rb[i].wait_recv()
        b["ra_out"][i] = mm(b["turn"][...], b["rb_in"][i].reshape(R, N)).astype(bf16).reshape(NG, 16, N)
        ex_ra[i].start()
        b["ra_in"][i, g] = b["ra_out"][i, g]

    for i in range(2):
        ex_b[i].wait_recv()
        forward(b["b_in"][i].reshape(R, N).astype(f32), wt2["w"], g2, s2, i, False)
        spread_heads(s2["q"][i], s2["qs"].at[i])
        back_values(s2, i)
        back_heads(s2, i)
        dx = back_input(b["upper"][i], wt2["wT"], g2, s2, i)
        b["rb_out"][i] = dx.astype(bf16).reshape(NR, 2, 16, N)
        ex_rb[i].start()
        b["rb_in"][i, r] = b["rb_out"][i, r]

    def output_weights(s, top):
        return mm(s["combT"][0].astype(bf16), top[0]) + mm(s["combT"][1].astype(bf16), top[1])

    sum_inter.put(3, output_weights(s2, b["upper"]))
    proj = mm(s2["hiddenT"][...], s2["gqkv"][...])
    for j in range(3):
        sum_inter.put(j, proj[:, j * N : (j + 1) * N])
    sum_inter.first()
    turn(0)
    sum_inter.second()
    turn(1)

    for i in range(2):
        ex_ra[i].wait_recv()
    came = b["ra_in"][...].reshape(2 * R, N)
    for c in range(2):
        b["top"][c] = mm(b["gather"][c], came).astype(bf16)
    for c in range(2):
        back_start(b["top"][c], wt1["w3T"], s1, c)
        back_values(s1, c)
    sum_early.put(0, mm(s1["hiddenT"][...], s1["gqkv"][:, 2 * N : 3 * N]))
    sum_early.put(1, output_weights(s1, b["top"]))
    sum_early.first()
    sum_inter.third()
    back_heads(s1, 1)
    sum_early.second()
    back_heads(s1, 0)
    proj = mm(s1["hiddenT"][...], s1["gqkv"][:, 0 : 2 * N])
    for j in range(2):
        sum_late.put(j, proj[:, j * N : (j + 1) * N])
    sum_late.first()
    dx1 = back_input(b["top"][1], wt1["wT"], g1, s1, 1)
    b["tail"][...] = dx1[R // 2 :].astype(bf16)
    tail = copy("tail", 0, b["tail"], b["tail_in"], {"seq": right})
    tail = Single(tail, tail)
    tail.start()
    sum_late.second()
    dx0 = back_input(b["top"][0], wt1["wT"], g1, s1, 0)
    sum_early.third()
    sum_late.third()
    sum_inter.fourth()
    sum_early.fourth()
    tail.wait_recv()
    carried = jnp.where(me > 0, b["tail_in"][...].astype(f32), 0.0)
    gf[0, 0 : R // 2] = (dx0[0 : R // 2] + carried).astype(bf16)
    gf[0, R // 2 :] = (dx0[R // 2 :] + dx1[0 : R // 2]).astype(bf16)
    sum_late.fourth()
    sum_inter.fifth()
    sum_early.fifth()

    def gain_sum(l, w, gw):
        total = w[0].astype(f32) * gw[0].astype(f32)
        for j in range(1, 3):
            total += w[j].astype(f32) * gw[j].astype(f32)
        rows = jnp.broadcast_to(jnp.sum(total, -1, keepdims=True), (N, 128))
        gg[l : l + 1] = rows.T[0:1] / b["gains"][l : l + 1]

    sum_inter.finish(gw2, 0)
    gain_sum(1, wt2["w"], gw2)
    sum_early.finish(gw1, 2)
    sum_late.fifth()
    sum_late.finish(gw1, 0)
    gain_sum(0, wt1["w"], gw1)

    for ex in Exchange.started:
        ex.wait_send()


def widen(gf, gw1, gw2, gg, gf_out, gw1_out, gw2_out, gg_out):
    gw1_out[...] = gw1[...].astype(f32)
    gw2_out[...] = gw2[...].astype(f32)
    gf_out[...] = gf[...]
    gg_out[...] = gg[...]


def on_device(n_seq, frames, upstream, w1, w2, gains):
    vmem = pl.BlockSpec(memory_space=pltpu.VMEM)
    bufs, sems = comm_scratch()

    def shapes(kind):
        return [
            jax.ShapeDtypeStruct(frames.shape, bf16),
            jax.ShapeDtypeStruct(w1.shape, kind),
            jax.ShapeDtypeStruct(w2.shape, kind),
            jax.ShapeDtypeStruct(gains.shape, f32),
        ]

    found = pl.pallas_call(
        functools.partial(kernel, n_seq),
        in_specs=[pl.BlockSpec(memory_space=pl.ANY)] * 5,
        out_specs=[vmem] * 4,
        out_shape=shapes(bf16),
        scratch_shapes=[
            saved_scratch(),
            saved_scratch(),
            shared_scratch(),
            weight_scratch(),
            weight_scratch(),
            bufs,
            sems,
        ],
        compiler_params=pltpu.CompilerParams(
            collective_id=0, has_side_effects=True, vmem_limit_bytes=56 * 2**20
        ),
        name="block_backward",
    )(frames, upstream, w1, w2, gains)
    return pl.pallas_call(
        widen,
        in_specs=[vmem] * 4,
        out_specs=[vmem] * 4,
        out_shape=shapes(f32),
        compiler_params=pltpu.CompilerParams(vmem_limit_bytes=60 * 2**20),
        name="widen",
    )(*found)


def solution(mesh):
    placed = (P("dp", "seq", None), P("dp", "seq", None, None), P(), P(), P())
    return jax.shard_map(
        functools.partial(on_device, mesh.shape["seq"]),
        mesh=mesh,
        in_specs=placed,
        out_specs=(P("dp", "seq", None), P(), P(), P()),
        check_vma=False,
    )
```
